256 devices in a mesh: pipe: 16 (over y, z_lo, core), expert: 16 (over z_hi, x).
Axes of the slice: x: 4, y: 4, z: 8 (z_hi: 4, z_lo: 2; z = z_hi * 2 + z_lo), core: 2. Of those that a mesh axis runs over, the one named last changes fastest.
Arguments:
- forward_input: bfloat16 [16, 1024, 3584], P('pipe', 'expert'), may hold values from -6 to 6
- forward_route: int32 [16, 1024, 1], P('pipe', 'expert'), may hold values from 0 to 1; in each aligned block of 64 rows (0 to 63, 64 to 127, ..., all dimensions but the last counted through in order) at most 34 rows name the same one
- forward_weight: float32 [16, 1024], P('pipe', 'expert'), may hold values from 0.25 to 1
- backward_grad: bfloat16 [16, 1024, 3584], P('pipe', 'expert'), may hold values from -6 to 6
- backward_route: int32 [16, 1024, 1], P('pipe', 'expert'), may hold values from 0 to 1; in each aligned block of 64 rows (0 to 63, 64 to 127, ..., all dimensions but the last counted through in order) at most 34 rows name the same one
- backward_weight: float32 [16, 1024], P('pipe', 'expert'), may hold values from 0.25 to 1
- saved_hidden: bfloat16 [16, 2, 16, 34, 2048], P('pipe', None, None, None, 'expert'), may hold values from -6 to 6
- gate_weight: bfloat16 [16, 3584, 2048], P('pipe', None, 'expert'), may hold values from -0.09375 to 0.09375
- up_weight: bfloat16 [16, 3584, 2048], P('pipe', None, 'expert'), may hold values from -0.09375 to 0.09375
- down_weight: bfloat16 [16, 2048, 3584], P('pipe', 'expert'), may hold values from -0.1875 to 0.1875
Outputs:
- forward_output: bfloat16 [16, 1024, 3584], P('pipe', 'expert')
- input_grad: bfloat16 [16, 1024, 3584], P('pipe', 'expert')
The draws below stay inside these ranges and needn't reach their ends.
Inputs may be any that keep to these rules, and one draw needn't show every extreme that they name: `forward_route`: within each device's 64 tokens at most 34 choose any one expert; in some blocks one expert is chosen by exactly 34. `backward_route`: within each device's 64 tokens at most 34 choose any one expert; in some blocks one expert is chosen by exactly 34.
All inputs are finite; a program needn't handle non-finite values.
Results may differ from the reference program's by a relative error of at most 0.0064.
Values may be sent and summed in bfloat16 or wider, within the bound.
A program may use at most 128 MiB of HBM per device.

```python
import math
import jax
import jax.numpy as jnp
import numpy as np
from jax import lax

D = 3584
FF = 1024
EXPERTS = 2
TOK_DEV = 64
CAP = 34
SPLIT = 8
UNITS = 128
TOKENS = 1024
SECTIONS = 16
N_EXPERT = 16


def block_scale(rng, extent, pieces, smallest, largest):
    level, own = 1.0, jax.random.fold_in(rng, 6)
    for dim, blocks in pieces:
        draws = jnp.exp(jax.random.uniform(jax.random.fold_in(own, dim), (blocks,), jnp.float32, smallest / len(pieces), largest / len(pieces)))
        level = level * jnp.repeat(draws, extent[dim] // blocks).reshape([-1 if axis == dim else 1 for axis in range(len(extent))])
    return level


def shared_out(rng, own, number, rows, count, top, limit, slope):
    ranking = jax.random.permutation(rng, count)
    heavy_load, ordinary = load_shares(count, rows * top, limit, slope, True), load_shares(count, rows * top, limit, slope, False)
    places = jnp.arange(count)

    def named(tallies, rotation):
        used = int((tallies > 0).sum())
        fixed = max(1, used // 4)
        moved = fixed + (places - fixed + rotation * (used - fixed)) % max(1, count - fixed)
        return jnp.zeros((count,), jnp.int32).at[ranking[jnp.where(places < fixed, places, moved)]].set(jnp.asarray(tallies, jnp.int32))

    tallies = jnp.where(number % 4 == 0, named(heavy_load, number // 4), named(ordinary, number - number // 4 - 1))
    mixed = jax.random.permutation(jax.random.fold_in(own, 3), count)
    source_of, sink = mixed[0:count // 2 * 2:2], mixed[1:count // 2 * 2:2]
    room = jnp.minimum(tallies[source_of] - 1, limit - tallies[sink]) // 2
    room = jnp.where((source_of == ranking[0]) | (sink == ranking[0]) | (tallies[sink] == 0), 0, jnp.maximum(room, 0))
    moved = jax.random.randint(jax.random.fold_in(own, 4), (count // 2,), 0, 1 << 20) % (room + 1)
    tallies = tallies.at[source_of].add(-moved).at[sink].add(moved)
    members = jnp.searchsorted(jnp.cumsum(tallies), jnp.arange(rows * top), side="right").astype(jnp.int32)
    listing = members.reshape(top, rows).T
    listing = listing[jax.random.permutation(jax.random.fold_in(own, 1), rows)]
    rotation = jax.random.randint(jax.random.fold_in(own, 2), (rows, 1), 0, top)
    return jnp.take_along_axis(listing, (jnp.arange(top)[None, :] + rotation) % top, axis=1)


def load_shares(amount, total, limit, slope, full):
    loads = [(1 << 20) // math.isqrt(rank ** slope) + 1 for rank in range(1, amount + 1)]
    largest = limit if full else min(limit, max(-(-total // amount), total * loads[0] // sum(loads)))
    least = 1 if total - largest >= amount - 1 else 0
    counts, spare = [largest] + [least] * (amount - 1), total - largest - least * (amount - 1)
    while spare > 0:
        free = [i for i in range(1, amount) if counts[i] < largest] or [i for i in range(1, amount) if counts[i] < limit]
        mass, remaining = sum([loads[i] for i in free]), spare
        for i in free:
            extra = min(limit - counts[i], max(1, remaining * loads[i] // mass), spare)
            counts[i] = counts[i] + extra
            spare = spare - extra
    return np.array(counts)


def bell_draw(stream_key, extent, width, most, cuts=(), kind=jnp.bfloat16):
    array = jax.random.normal(stream_key, extent, jnp.float32) * width
    if len(cuts) > 0:
        array = block_scale(stream_key, extent, cuts, -0.22, 0.18) * array
    return jnp.clip(array, min=-most, max=most).astype(kind)


def setup_inputs(seed: int = 0) -> dict:
    key_list = jax.random.split(jax.random.key(seed), 11)
    forward_input = bell_draw(key_list[0], (SECTIONS, TOKENS, D), 1.0, 6.0, ((0, 16), (1, 16)))
    forward_route_keys = jax.random.split(jax.random.fold_in(key_list[1], 1), SECTIONS * TOKENS // TOK_DEV)
    forward_route_turns = jax.random.permutation(jax.random.fold_in(key_list[1], 3), SECTIONS * TOKENS // TOK_DEV)
    forward_route = jax.vmap(lambda own, number: shared_out(jax.random.fold_in(key_list[1], 2), own, number, TOK_DEV, EXPERTS, 1, CAP, 1))(forward_route_keys, forward_route_turns).reshape((SECTIONS, TOKENS, 1))
    forward_weight = jnp.clip(0.25 + 0.75 * jax.random.uniform(key_list[2], (SECTIONS, TOKENS), jnp.float32) ** block_scale(key_list[2], (SECTIONS, TOKENS), ((0, 16), (1, 16)), -0.2, 0.2), 0.25, 1.0)
    backward_grad = bell_draw(key_list[3], (SECTIONS, TOKENS, D), 1.0, 6.0, ((0, 16), (1, 16)))
    backward_route_keys = jax.random.split(jax.random.fold_in(key_list[4], 1), SECTIONS * TOKENS // TOK_DEV)
    backward_route_turns = jax.random.permutation(jax.random.fold_in(key_list[4], 3), SECTIONS * TOKENS // TOK_DEV)
    backward_route = jax.vmap(lambda own, number: shared_out(jax.random.fold_in(key_list[4], 2), own, number, TOK_DEV, EXPERTS, 1, CAP, 1))(backward_route_keys, backward_route_turns).reshape((SECTIONS, TOKENS, 1))
    backward_weight = jnp.clip(0.25 + 0.75 * jax.random.uniform(key_list[5], (SECTIONS, TOKENS), jnp.float32) ** block_scale(key_list[5], (SECTIONS, TOKENS), ((0, 16), (1, 16)), -0.2, 0.2), 0.25, 1.0)
    saved_hidden = bell_draw(key_list[6], (SECTIONS, 2, N_EXPERT, CAP, EXPERTS * FF), 1.5, 6.0, ((0, 16), (4, 16)))
    gate_weight = bell_draw(key_list[7], (SECTIONS, D, EXPERTS * FF), D ** -0.5, 0.09375, ((0, 16), (2, 16)))
    up_weight = bell_draw(key_list[8], (SECTIONS, D, EXPERTS * FF), D ** -0.5, 0.09375, ((0, 16), (2, 16)))
    down_weight = bell_draw(key_list[9], (SECTIONS, EXPERTS * FF, D), FF ** -0.5, 0.1875, ((0, 16), (1, 16)))
    return dict(forward_input=forward_input, forward_route=forward_route, forward_weight=forward_weight, backward_grad=backward_grad, backward_route=backward_route, backward_weight=backward_weight, saved_hidden=saved_hidden, gate_weight=gate_weight, up_weight=up_weight, down_weight=down_weight)


def select_rows(route_block, value_block):
    onehot = (route_block[:, :, None] == jnp.arange(EXPERTS, dtype=jnp.int32)[None, None, :]).astype(jnp.int32)
    before = (jnp.cumsum(onehot, axis=1) - onehot).astype(jnp.int32)
    slot_of = jnp.sum(before * onehot, axis=2).astype(jnp.int32)
    flat_slot = (route_block * CAP + slot_of).astype(jnp.int32)
    picker = (flat_slot[:, None, :] == jnp.arange(EXPERTS * CAP, dtype=jnp.int32)[None, :, None]).astype(jnp.float32)
    picked = jnp.einsum("jrt,jtd->jrd", picker, value_block.astype(jnp.float32))
    return flat_slot, picked.astype(jnp.bfloat16)


def rounded(value):
    return lax.optimization_barrier(value.astype(jnp.bfloat16)).astype(jnp.float32)


def take_rows(table, index):
    return jnp.take(table, index, axis=0)


def one_section(section_items):
    (forward_input, forward_route, forward_weight, backward_grad, backward_route,
     backward_weight, saved_hidden, gate_weight, up_weight, down_weight) = section_items
    holders = N_EXPERT
    rows_total = holders * CAP
    flat_fwd, rows_fwd = select_rows(forward_route[:, 0].reshape(holders, TOK_DEV),
                                     forward_input.reshape(holders, TOK_DEV, D))
    scaled = (backward_weight[:, None] * backward_grad.astype(jnp.float32)).astype(jnp.bfloat16)
    flat_bwd, rows_bwd = select_rows(backward_route[:, 0].reshape(holders, TOK_DEV),
                                     scaled.reshape(holders, TOK_DEV, D))
    outs_fwd = []
    outs_bwd = []
    for expert_id in range(EXPERTS):
        token_rows = rows_fwd[:, expert_id * CAP:(expert_id + 1) * CAP].reshape(rows_total, D)
        grad_rows_in = rows_bwd[:, expert_id * CAP:(expert_id + 1) * CAP].reshape(rows_total, D)
        total_fwd = jnp.zeros((rows_total, D), jnp.float32)
        total_bwd = jnp.zeros((rows_total, D), jnp.float32)
        for shard_id in range(SPLIT):
            first_col = expert_id * FF + shard_id * UNITS
            last_col = first_col + UNITS
            gate_cols = gate_weight[:, first_col:last_col]
            up_cols = up_weight[:, first_col:last_col]
            down_rows = down_weight[first_col:last_col]
            gate_pre = jnp.dot(token_rows, gate_cols, preferred_element_type=jnp.float32)
            up_pre = jnp.dot(token_rows, up_cols, preferred_element_type=jnp.float32)
            hidden = (jax.nn.silu(gate_pre) * up_pre).astype(jnp.bfloat16)
            total_fwd = total_fwd + rounded(jnp.dot(hidden, down_rows, preferred_element_type=jnp.float32))
            grad_hidden = jnp.dot(grad_rows_in, down_rows.T, preferred_element_type=jnp.float32)
            pre_gate = saved_hidden[0, :, :, first_col:last_col].reshape(rows_total, UNITS).astype(jnp.float32)
            pre_up = saved_hidden[1, :, :, first_col:last_col].reshape(rows_total, UNITS).astype(jnp.float32)
            sigmoid_gate = jax.nn.sigmoid(pre_gate)
            grad_gate = (grad_hidden * pre_up * sigmoid_gate * (1.0 + pre_gate * (1.0 - sigmoid_gate))).astype(jnp.bfloat16)
            grad_up = (grad_hidden * pre_gate * sigmoid_gate).astype(jnp.bfloat16)
            partial_value = jnp.dot(grad_gate, gate_cols.T, preferred_element_type=jnp.float32)
            partial_value = partial_value + jnp.dot(grad_up, up_cols.T, preferred_element_type=jnp.float32)
            total_bwd = total_bwd + rounded(partial_value)
        outs_fwd.append(total_fwd.reshape(holders, CAP, D))
        outs_bwd.append(total_bwd.reshape(holders, CAP, D))
    expert_fwd = jnp.stack(outs_fwd, axis=1).reshape(holders, EXPERTS * CAP, D)
    expert_bwd = jnp.stack(outs_bwd, axis=1).reshape(holders, EXPERTS * CAP, D)
    picked_fwd = jax.vmap(take_rows)(expert_fwd, flat_fwd)
    picked_bwd = jax.vmap(take_rows)(expert_bwd, flat_bwd)
    forward_token = (forward_weight.reshape(holders, TOK_DEV)[:, :, None] * picked_fwd).astype(jnp.bfloat16)
    grad_token = picked_bwd.astype(jnp.bfloat16)
    return forward_token.reshape(TOKENS, D), grad_token.reshape(TOKENS, D)


def reference(forward_input, forward_route, forward_weight, backward_grad, backward_route,
              backward_weight, saved_hidden, gate_weight, up_weight, down_weight):
    forward_all, grads_all = lax.map(one_section, (forward_input, forward_route, forward_weight,
                                                 backward_grad, backward_route, backward_weight,
                                                 saved_hidden, gate_weight, up_weight, down_weight))
    return jnp.roll(forward_all, 1, axis=0), jnp.roll(grads_all, -1, axis=0)
```

```python
import jax
import jax.numpy as jnp
from jax import lax
from jax.experimental import pallas as pl
from jax.experimental.pallas import tpu as pltpu
from jax.sharding import PartitionSpec as P

MESH = pl.DeviceIdType.MESH
BF16 = jnp.bfloat16
F32 = jnp.float32
CAP = 34
TOK = 64
D = 3584
UNITS = 128
BLK = 512
NBLK = D // BLK
GROUPS = ((0, 2), (2, 4), (4, 6), (6, 7))
NG = len(GROUPS)
FWD, BWD = 0, 1


def iota(shape, dim):
    return lax.broadcasted_iota(jnp.int32, shape, dim)


def dot(a, b):
    return jnp.dot(a, b, preferred_element_type=F32)


def dot_t(a, b):
    return lax.dot_general(a, b, (((1,), (1,)), ((), ())), preferred_element_type=F32)


def group_cols(g):
    first, last = GROUPS[g]
    return pl.ds(first * BLK, (last - first) * BLK)


def block_cols(c):
    return pl.ds(c * BLK, BLK)


def row_index(route):
    route = jnp.broadcast_to(route, (TOK, 128))
    to_one = (route == 1).astype(F32)
    earlier = (iota((TOK, TOK), 1) < iota((TOK, TOK), 0)).astype(BF16)
    ones_before = dot(earlier, to_one.astype(BF16))
    place = iota((TOK, 128), 0).astype(F32)
    return jnp.where(route == 1, CAP + ones_before, place - ones_before)


def tokens_in_lanes(index):
    diagonal = iota((TOK, TOK), 0) == iota((TOK, TOK), 1)
    spread = jnp.where(diagonal, index[:, :TOK], 0.0).astype(BF16)
    return dot(jnp.ones((TOK, TOK), BF16), spread)


def unpack_extra(c):
    row, col = iota((16, 128), 0), iota((16, 128), 1)
    return (((col >> 4) == (row >> 1)) & ((col & 15) == 2 * c + (row & 1))).astype(BF16)


def pack_extra(c):
    row, col = iota((128, 16), 0), iota((128, 16), 1)
    return (((row >> 4) == (col >> 1)) & ((row & 15) == 2 * c + (col & 1))).astype(BF16)


def kernel(
    fi, fr, fw, bg, br, bw, saved, gate, up, down,
    out_f, out_b,
    gw, uw, dw, sv,
    ds_main, ds_extra, tok, tok_extra,
    info_s, info_r,
    acc_a, acc_b, act_a, act_b,
    own, own_extra,
    xs, xs_extra, xr, xr_extra,
    zs, zs_extra, zr, zr_extra,
    loc_sem,
    w_send, w_recv, i_send, i_recv,
    zd_send, zd_recv, xd_send, xd_recv,
    xc_send, xc_recv, zc_send, zc_recv,
):
    p = lax.axis_index("pipe")
    e = lax.axis_index("expert")
    z, x = e // 4, e % 4
    turn = 1 - 2 * ((x + p) % 2)
    x_w = (x + turn + 4) % 4
    x_t = (x - turn + 4) % 4
    x_far = (x + 2) % 4
    weight_peer = (p, z * 4 + x_w)
    token_peer = (p, z * 4 + x_t)
    after, before = (p + 1) % 16, (p + 15) % 16

    barrier = pltpu.get_barrier_semaphore()
    peers = [weight_peer, token_peer]
    peers += [(p, ((z + dz) % 4) * 4 + x) for dz in range(1, 4)]
    peers += [(q, ((z + dz) % 4) * 4 + x) for q in (after, before) for dz in range(4)]
    for peer in peers:
        pl.semaphore_signal(barrier, inc=1, device_id=peer, device_id_type=MESH)

    sends = []

    def remote(src, dst, send, recv, peer):
        copy = pltpu.make_async_remote_copy(
            src_ref=src, dst_ref=dst, send_sem=send, recv_sem=recv,
            device_id=peer, device_id_type=MESH,
        )
        copy.start()
        sends.append(copy)
        return copy

    local = [
        pltpu.make_async_copy(gate.at[0], gw.at[:, pl.ds(0, UNITS)], loc_sem.at[0]),
        pltpu.make_async_copy(up.at[0], uw.at[:, pl.ds(0, UNITS)], loc_sem.at[1]),
        pltpu.make_async_copy(down.at[0], dw.at[pl.ds(0, UNITS)], loc_sem.at[2]),
        pltpu.make_async_copy(saved.at[:, :, x], sv.at[0, 0], loc_sem.at[3]),
        pltpu.make_async_copy(saved.at[:, :, x_t], sv.at[0, 1], loc_sem.at[4]),
    ]
    for copy in local:
        copy.start()

    index_f = row_index(fr[0])
    index_b = row_index(br[0])
    info_s[BWD] = index_b
    weight_spread = jnp.where(
        iota((TOK, TOK), 0) == iota((TOK, TOK), 1), jnp.broadcast_to(fw[...], (TOK, TOK)), 0.0
    )
    weight_col = jnp.sum(weight_spread, axis=1, keepdims=True)
    info_s[FWD] = jnp.where(
        iota((TOK, 128), 1) == 1, jnp.broadcast_to(weight_col, (TOK, 128)), index_f
    )
    grad_spread = jnp.where(
        iota((TOK, TOK), 0) == iota((TOK, TOK), 1), jnp.broadcast_to(bw[...], (TOK, TOK)), 0.0
    )
    grad_col = jnp.sum(grad_spread, axis=1, keepdims=True)

    def pick(mb, index, read):
        by_lane = tokens_in_lanes(index)
        row = iota((TOK, TOK), 0)
        picker = (by_lane == ((row >> 5) * CAP + (row & 31)).astype(F32)).astype(BF16)
        row = iota((32, TOK), 0)
        extra_id = (row >> 4) * CAP + 32 + (row & 1)
        extra = jnp.zeros((32, BLK), F32)
        for c in range(NBLK):
            values = read(c)
            picked = dot(picker, values).astype(BF16)
            ds_main[mb, 0, :, block_cols(c)] = picked[:32]
            ds_main[mb, 1, :, block_cols(c)] = picked[32:]
            wanted = jnp.where(((row & 15) >> 1) == c, extra_id, -1).astype(F32)
            extra += dot((by_lane[:32] == wanted).astype(BF16), values)
        extra = extra.astype(BF16)
        ds_extra[mb, 0] = extra[:16]
        ds_extra[mb, 1] = extra[16:]
        tok[mb, 0, z] = ds_main[mb, z // 2]
        tok_extra[mb, 0, z] = ds_extra[mb, z // 2]

    def read_grad(c):
        return (grad_col * bg[0, :, block_cols(c)].astype(F32)).astype(BF16)

    def read_input(c):
        return fi[0, :, block_cols(c)]

    zd = {}
    xd = {}

    def send_rows(mb):
        for g in (NG, *range(NG)):
            for dz in (2, 1, 3):
                tz = (z + dz) % 4
                if g == NG:
                    src, dst = ds_extra.at[mb, tz // 2], tok_extra.at[mb, 0, z]
                else:
                    src = ds_main.at[mb, tz // 2, :, group_cols(g)]
                    dst = tok.at[mb, 0, z, :, group_cols(g)]
                zd[mb, g, dz] = remote(
                    src, dst, zd_send.at[mb, g, dz - 1], zd_recv.at[mb, g, dz - 1],
                    (p, tz * 4 + x),
                )

    def pass_rows(mb, g):
        for dz in range(1, 4):
            zd[mb, g, dz].wait_recv()
        if g == NG:
            src, dst = tok_extra.at[mb, 0], tok_extra.at[mb, 1]
        else:
            src = tok.at[mb, 0, :, :, group_cols(g)]
            dst = tok.at[mb, 1, :, :, group_cols(g)]
        xd[mb, g] = remote(src, dst, xd_send.at[mb, g], xd_recv.at[mb, g], token_peer)

    pick(BWD, index_b, read_grad)
    pl.semaphore_wait(barrier, len(peers))

    from_down = remote(down.at[0], dw.at[pl.ds(UNITS, UNITS)], w_send.at[0], w_recv.at[0], weight_peer)
    from_saved = [
        remote(saved.at[:, :, x_w], sv.at[1, 0], w_send.at[1], w_recv.at[1], weight_peer),
        remote(saved.at[:, :, x_far], sv.at[1, 1], w_send.at[2], w_recv.at[2], weight_peer),
    ]
    send_rows(BWD)
    infos = [
        remote(info_s.at[FWD], info_r.at[FWD], i_send.at[FWD], i_recv.at[FWD], (after, e)),
        remote(info_s.at[BWD], info_r.at[BWD], i_send.at[BWD], i_recv.at[BWD], (before, e)),
    ]
    pick(FWD, index_f, read_input)
    send_rows(FWD)

    for g in (NG, *range(NG)):
        pass_rows(BWD, g)

    from_gate, from_up = [], []
    for g in range(NG):
        cols = group_cols(g)
        from_gate.append(remote(
            gate.at[0, cols], gw.at[cols, pl.ds(UNITS, UNITS)], w_send.at[3 + g], w_recv.at[3 + g], weight_peer))
        from_up.append(remote(
            up.at[0, cols], uw.at[cols, pl.ds(UNITS, UNITS)], w_send.at[3 + NG + g], w_recv.at[3 + NG + g], weight_peer))

    def rows_of(mb, c):
        main = tok[mb, :, :, :, block_cols(c)].reshape(256, BLK)
        extra = dot(unpack_extra(c), tok_extra[mb].reshape(128, BLK)).astype(BF16)
        return jnp.concatenate([main, extra], axis=0)

    for copy in local:
        copy.wait()
    from_down.wait_recv()
    acc_a[...] = jnp.zeros_like(acc_a)
    xd[BWD, NG].wait_recv()
    for g in range(NG):
        xd[BWD, g].wait_recv()
        for c in range(*GROUPS[g]):
            acc_a[...] += dot_t(rows_of(BWD, c), dw[:, block_cols(c)])
    for copy in from_saved:
        copy.wait_recv()

    def saved_rows(kind, h):
        main = sv[h, :, kind, :, 0:32, :].reshape(256, UNITS).astype(F32)
        extra = [sv[h, w, kind, s, 32:34, :].astype(F32) for w in range(2) for s in range(4)]
        return jnp.concatenate([main, *extra], axis=0)

    for h in range(2):
        lanes = pl.ds(h * UNITS, UNITS)
        g_pre, u_pre = saved_rows(0, h), saved_rows(1, h)
        sig = jax.nn.sigmoid(g_pre)
        grad = acc_a[:, lanes]
        act_a[:, lanes] = (grad * u_pre * sig * (1.0 + g_pre * (1.0 - sig))).astype(BF16)
        act_b[:, lanes] = (grad * g_pre * sig).astype(BF16)

    xc, zc = {}, {}

    def keep(mb, c, value):
        own[:, block_cols(c)] = value[:128]
        xs[mb, :, :, block_cols(c)] = value[128:256].astype(BF16).reshape(4, 32, BLK)
        own_extra[...] += dot(pack_extra(c), value[256:].astype(BF16))

    def send_part(mb, g):
        if g == NG:
            xs_extra[mb] = own_extra[64:].astype(BF16).reshape(4, 16, BLK)
            src, dst = xs_extra.at[mb], xr_extra.at[mb]
        else:
            src, dst = xs.at[mb, :, :, group_cols(g)], xr.at[mb, :, :, group_cols(g)]
        xc[mb, g] = remote(src, dst, xc_send.at[mb, g], xc_recv.at[mb, g], token_peer)

    def send_sum(mb, g):
        section = after if mb == FWD else before
        xc[mb, g].wait_recv()
        if g == NG:
            zs_extra[mb] = (own_extra[:64].reshape(4, 16, BLK) + xr_extra[mb].astype(F32)).astype(BF16)
        else:
            for c in range(*GROUPS[g]):
                cols = block_cols(c)
                zs[mb, :, :, cols] = (
                    own[:, cols].reshape(4, 32, BLK) + xr[mb, :, :, cols].astype(F32)
                ).astype(BF16)
        for dz in (2, 1, 3, 0):
            tz = (z + dz) % 4
            if g == NG:
                src, dst = zs_extra.at[mb, tz], zr_extra.at[mb, z]
            else:
                src, dst = zs.at[mb, tz, :, group_cols(g)], zr.at[mb, z, :, group_cols(g)]
            zc[mb, g, dz] = remote(
                src, dst, zc_send.at[mb, g, dz], zc_recv.at[mb, g, dz], (section, tz * 4 + x))

    own_extra[...] = jnp.zeros_like(own_extra)
    pass_rows(FWD, NG)
    for g in range(NG):
        pass_rows(FWD, g)
        from_gate[g].wait_recv()
        from_up[g].wait_recv()
        for c in range(*GROUPS[g]):
            rows = block_cols(c)
            keep(BWD, c, dot_t(act_a[...], gw[rows]) + dot_t(act_b[...], uw[rows]))
        send_part(BWD, g)
        if g > 0:
            send_sum(BWD, g - 1)
    send_part(BWD, NG)
    send_sum(BWD, NG - 1)
    send_sum(BWD, NG)

    acc_a[...] = jnp.zeros_like(acc_a)
    acc_b[...] = jnp.zeros_like(acc_b)
    xd[FWD, NG].wait_recv()
    for g in range(NG):
        xd[FWD, g].wait_recv()
        for c in range(*GROUPS[g]):
            rows = rows_of(FWD, c)
            acc_a[...] += dot(rows, gw[block_cols(c)])
            acc_b[...] += dot(rows, uw[block_cols(c)])
    act_a[...] = (jax.nn.silu(acc_a[...]) * acc_b[...]).astype(BF16)
    own_extra[...] = jnp.zeros_like(own_extra)
    for g in range(NG):
        for c in range(*GROUPS[g]):
            keep(FWD, c, dot(act_a[...], dw[:, block_cols(c)]))
        send_part(FWD, g)
        if g > 0:
            send_sum(FWD, g - 1)
    send_part(FWD, NG)
    send_sum(FWD, NG - 1)
    send_sum(FWD, NG)

    def place(mb, out):
        infos[mb].wait_recv()
        info = info_r[mb]
        index = info[:, 0:1]
        col = iota((TOK, 128), 1)
        whole = (index == ((col >> 6) * CAP + (col & 31)).astype(F32)).astype(BF16)
        col = iota((TOK, TOK), 1)
        extra_id = (col >> 5) * CAP + 32 + (col & 1)
        for g in (NG, *range(NG)):
            for dz in range(4):
                zc[mb, g, dz].wait_recv()
            if g == NG:
                continue
            for c in range(*GROUPS[g]):
                wanted = jnp.where(((col & 15) >> 1) == c, extra_id, -1).astype(F32)
                value = dot(whole, zr[mb, :, :, block_cols(c)].reshape(128, BLK))
                value += dot((index == wanted).astype(BF16), zr_extra[mb].reshape(64, BLK))
                if mb == FWD:
                    value = info[:, 1:2] * value
                out[0, :, block_cols(c)] = value.astype(BF16)

    place(BWD, out_b)
    place(FWD, out_f)
    for copy in sends:
        copy.wait_send()


def per_device(fi, fr, fw, bg, br, bw, saved, gate, up, down):
    vmem = pl.BlockSpec(memory_space=pltpu.VMEM)
    anywhere = pl.BlockSpec(memory_space=pl.ANY)
    dma = pltpu.SemaphoreType.DMA
    rows_out = jax.ShapeDtypeStruct((1, TOK, D), BF16)
    saved = saved[0].reshape(2, 4, 4, CAP, UNITS)
    return pl.pallas_call(
        kernel,
        out_shape=(rows_out, rows_out),
        in_specs=[vmem] * 6 + [anywhere] * 4,
        out_specs=(vmem, vmem),
        scratch_shapes=[
            pltpu.VMEM((D, 2 * UNITS), BF16),
            pltpu.VMEM((D, 2 * UNITS), BF16),
            pltpu.VMEM((2 * UNITS, D), BF16),
            pltpu.VMEM((2, 2, 2, 4, CAP, UNITS), BF16),
            pltpu.VMEM((2, 2, 32, D), BF16),
            pltpu.VMEM((2, 2, 16, BLK), BF16),
            pltpu.VMEM((2, 2, 4, 32, D), BF16),
            pltpu.VMEM((2, 2, 4, 16, BLK), BF16),
            pltpu.VMEM((2, TOK, 128), F32),
            pltpu.VMEM((2, TOK, 128), F32),
            pltpu.VMEM((272, 256), F32),
            pltpu.VMEM((272, 256), F32),
            pltpu.VMEM((272, 256), BF16),
            pltpu.VMEM((272, 256), BF16),
            pltpu.VMEM((128, D), F32),
            pltpu.VMEM((128, BLK), F32),
            pltpu.VMEM((2, 4, 32, D), BF16),
            pltpu.VMEM((2, 4, 16, BLK), BF16),
            pltpu.VMEM((2, 4, 32, D), BF16),
            pltpu.VMEM((2, 4, 16, BLK), BF16),
            pltpu.VMEM((2, 4, 32, D), BF16),
            pltpu.VMEM((2, 4, 16, BLK), BF16),
            pltpu.VMEM((2, 4, 32, D), BF16),
            pltpu.VMEM((2, 4, 16, BLK), BF16),
            dma((5,)),
            dma((3 + 2 * NG,)),
            dma((3 + 2 * NG,)),
            dma((2,)),
            dma((2,)),
            dma((2, NG + 1, 3)),
            dma((2, NG + 1, 3)),
            dma((2, NG + 1)),
            dma((2, NG + 1)),
            dma((2, NG + 1)),
            dma((2, NG + 1)),
            dma((2, NG + 1, 4)),
            dma((2, NG + 1, 4)),
        ],
        compiler_params=pltpu.CompilerParams(
            collective_id=0, has_side_effects=True, vmem_limit_bytes=48 * 2**20
        ),
        name="routed_experts",
    )(fi, fr, fw, bg, br, bw, saved, gate, up, down)


def solution(mesh):
    placed = (
        P("pipe", "expert", None),
        P("pipe", "expert", None),
        P("pipe", "expert"),
        P("pipe", "expert", None),
        P("pipe", "expert", None),
        P("pipe", "expert"),
        P("pipe", None, None, None, "expert"),
        P("pipe", None, "expert"),
        P("pipe", None, "expert"),
        P("pipe", "expert", None),
    )
    return jax.shard_map(
        per_device,
        mesh=mesh,
        in_specs=placed,
        out_specs=(P("pipe", "expert", None), P("pipe", "expert", None)),
        check_vma=False,
    )
```

```python
import jax
import jax.numpy as jnp
from jax import lax
from jax.experimental import pallas as pl
from jax.experimental.pallas import tpu as pltpu
from jax.sharding import PartitionSpec as P

MESH = pl.DeviceIdType.MESH
BF16 = jnp.bfloat16
F32 = jnp.float32
CAP = 34
TOK = 64
D = 3584
UNITS = 128
BLK = 512
NBLK = D // BLK
GROUPS = ((0, 2), (2, 4), (4, 6), (6, 7))
NG = len(GROUPS)
FWD, BWD = 0, 1
Z_LAG = 2
W_AHEAD = 4


def iota(shape, dim):
    return lax.broadcasted_iota(jnp.int32, shape, dim)


def dot(a, b):
    return jnp.dot(a, b, preferred_element_type=F32)


def dot_t(a, b):
    return lax.dot_general(a, b, (((1,), (1,)), ((), ())), preferred_element_type=F32)


def group_cols(g):
    first, last = GROUPS[g]
    return pl.ds(first * BLK, (last - first) * BLK)


def block_cols(c):
    return pl.ds(c * BLK, BLK)


def column(values):
    diagonal = iota((TOK, TOK), 0) == iota((TOK, TOK), 1)
    spread = jnp.where(diagonal, jnp.broadcast_to(values.astype(F32), (TOK, TOK)), 0.0)
    return jnp.broadcast_to(jnp.sum(spread, axis=1, keepdims=True), (TOK, 128))


def row_index(route):
    to_one = (route == 1).astype(F32)
    earlier = (iota((TOK, TOK), 1) < iota((TOK, TOK), 0)).astype(BF16)
    ones_before = dot(earlier, to_one.astype(BF16))
    place = iota((TOK, 128), 0).astype(F32)
    return jnp.where(route == 1, CAP + ones_before, place - ones_before)


def tokens_in_lanes(index):
    diagonal = iota((TOK, TOK), 0) == iota((TOK, TOK), 1)
    spread = jnp.where(diagonal, index[:, :TOK], 0.0).astype(BF16)
    return dot(jnp.ones((TOK, TOK), BF16), spread)


def unpack_extra(c):
    row, col = iota((16, 128), 0), iota((16, 128), 1)
    return (((col >> 4) == (row >> 1)) & ((col & 15) == 2 * c + (row & 1))).astype(BF16)


def pack_extra(c):
    row, col = iota((128, 16), 0), iota((128, 16), 1)
    return (((row >> 4) == (col >> 1)) & ((row & 15) == 2 * c + (col & 1))).astype(BF16)


def kernel(
    fi_in, fr_in, fw_in, bg_in, br_in, bw_in, saved, gate, up, down,
    out_f, out_b,
    fi, fr, fw, bg, br, bw,
    gw, uw, dw, sv, sv_rows,
    ds_main, ds_extra, tok, tok_extra,
    info_s, info_r,
    acc_a, acc_b, act_a, act_b,
    own, own_extra,
    xs, xs_extra, xr, xr_extra,
    zs, zs_extra, zr, zr_extra,
    loc_sem,
    w_send, w_recv, i_send, i_recv,
    zd_send, zd_recv, xd_send, xd_recv,
    xc_send, xc_recv, zc_send, zc_recv,
):
    p = lax.axis_index("pipe")
    e = lax.axis_index("expert")
    z, x = e // 4, e % 4
    turn = 1 - 2 * ((x + p) % 2)
    x_w = (x + turn + 4) % 4
    x_t = (x - turn + 4) % 4
    weight_peer = (p, z * 4 + x_w)
    token_peer = (p, z * 4 + x_t)
    after, before = (p + 1) % 16, (p + 15) % 16

    barrier = pltpu.get_barrier_semaphore()
    peers = [weight_peer, token_peer]
    peers += [(p, ((z + dz) % 4) * 4 + x) for dz in range(1, 4)]
    peers += [(q, ((z + dz) % 4) * 4 + x) for q in (after, before) for dz in range(4)]
    for peer in peers:
        pl.semaphore_signal(barrier, inc=1, device_id=peer, device_id_type=MESH)

    sends = []

    def remote(src, dst, send, recv, peer):
        copy = pltpu.make_async_remote_copy(
            src_ref=src, dst_ref=dst, send_sem=send, recv_sem=recv,
            device_id=peer, device_id_type=MESH,
        )
        copy.start()
        sends.append(copy)
        return copy

    small = [
        pltpu.make_async_copy(src, dst, loc_sem.at[4 + i])
        for i, (src, dst) in enumerate(
            ((br_in, br), (bw_in, bw), (bg_in, bg), (fr_in, fr), (fw_in, fw), (fi_in, fi))
        )
    ]
    for copy in small:
        copy.start()
    local = [
        pltpu.make_async_copy(gate.at[0], gw.at[:, pl.ds(0, UNITS)], loc_sem.at[0]),
        pltpu.make_async_copy(up.at[0], uw.at[:, pl.ds(0, UNITS)], loc_sem.at[1]),
        pltpu.make_async_copy(down.at[0], dw.at[pl.ds(0, UNITS)], loc_sem.at[2]),
        pltpu.make_async_copy(saved, sv.at[0], loc_sem.at[3]),
    ]
    for copy in local:
        copy.start()

    def read_grad(c):
        return (grad_col[:, :1] * bg[0, :, block_cols(c)].astype(F32)).astype(BF16)

    def read_input(c):
        return fi[0, :, block_cols(c)]

    def pick_main(mb, by_lane, read, g):
        row = iota((TOK, TOK), 0)
        picker = (by_lane == ((row >> 5) * CAP + (row & 31)).astype(F32)).astype(BF16)
        for c in range(*GROUPS[g]):
            picked = dot(picker, read(c)).astype(BF16)
            ds_main[mb, 0, :, block_cols(c)] = picked[:32]
            ds_main[mb, 1, :, block_cols(c)] = picked[32:]
        tok[mb, 0, z, :, group_cols(g)] = ds_main[mb, z // 2, :, group_cols(g)]

    def pick_extra(mb, by_lane, read):
        row = iota((32, TOK), 0)
        extra_id = (row >> 4) * CAP + 32 + (row & 1)
        extra = jnp.zeros((32, BLK), F32)
        for c in range(NBLK):
            wanted = jnp.where(((row & 15) >> 1) == c, extra_id, -1).astype(F32)
            extra += dot((by_lane[:32] == wanted).astype(BF16), read(c))
        extra = extra.astype(BF16)
        ds_extra[mb, 0] = extra[:16]
        ds_extra[mb, 1] = extra[16:]
        tok_extra[mb, 0, z] = ds_extra[mb, z // 2]

    zd = {}
    xd = {}

    def send_rows(mb, g):
        for dz in (2, 1, 3):
            tz = (z + dz) % 4
            if g == NG:
                src, dst = ds_extra.at[mb, tz // 2], tok_extra.at[mb, 0, z]
            else:
                src = ds_main.at[mb, tz // 2, :, group_cols(g)]
                dst = tok.at[mb, 0, z, :, group_cols(g)]
            zd[mb, g, dz] = remote(
                src, dst, zd_send.at[mb, g, dz - 1], zd_recv.at[mb, g, dz - 1],
                (p, tz * 4 + x),
            )

    def pass_rows(mb, g):
        for dz in range(1, 4):
            zd[mb, g, dz].wait_recv()
        if g == NG:
            src, dst = tok_extra.at[mb, 0], tok_extra.at[mb, 1]
        else:
            src = tok.at[mb, 0, :, :, group_cols(g)]
            dst = tok.at[mb, 1, :, :, group_cols(g)]
        xd[mb, g] = remote(src, dst, xd_send.at[mb, g], xd_recv.at[mb, g], token_peer)

    from_gate, from_up = [], []

    def send_weights(g):
        cols = group_cols(g)
        from_gate.append(remote(
            gate.at[0, cols], gw.at[cols, pl.ds(UNITS, UNITS)],
            w_send.at[2 + g], w_recv.at[2 + g], weight_peer))
        from_up.append(remote(
            up.at[0, cols], uw.at[cols, pl.ds(UNITS, UNITS)],
            w_send.at[2 + NG + g], w_recv.at[2 + NG + g], weight_peer))

    for copy in small[:3]:
        copy.wait()
    index_b = row_index(column(br[...]))
    grad_col = column(bw[...])
    info_s[BWD] = index_b
    lanes_b = tokens_in_lanes(index_b)
    pl.semaphore_wait(barrier, len(peers))

    from_down = remote(down.at[0], dw.at[pl.ds(UNITS, UNITS)], w_send.at[0], w_recv.at[0], weight_peer)
    from_saved = remote(saved, sv.at[1], w_send.at[1], w_recv.at[1], weight_peer)
    for g in range(NG):
        pick_main(BWD, lanes_b, read_grad, g)
        send_rows(BWD, g)
    pick_extra(BWD, lanes_b, read_grad)
    send_rows(BWD, NG)

    for copy in small[3:]:
        copy.wait()
    index_f = row_index(column(fr[...]))
    info_s[FWD] = jnp.where(iota((TOK, 128), 1) == 1, column(fw[...]), index_f)
    lanes_f = tokens_in_lanes(index_f)
    infos = [
        remote(info_s.at[FWD], info_r.at[FWD], i_send.at[FWD], i_recv.at[FWD], (after, e)),
        remote(info_s.at[BWD], info_r.at[BWD], i_send.at[BWD], i_recv.at[BWD], (before, e)),
    ]
    pick_extra(FWD, lanes_f, read_input)
    for g in range(NG):
        pick_main(FWD, lanes_f, read_input, g)

    forward_order = [NG, *range(NG)]
    for g in range(NG):
        pass_rows(BWD, g)
        if g >= Z_LAG:
            send_rows(FWD, forward_order[g - Z_LAG])
        if g == NG - 2:
            send_weights(0)
    pass_rows(BWD, NG)
    for g in forward_order[max(NG - Z_LAG, 0):]:
        send_rows(FWD, g)
    for g in range(1, W_AHEAD):
        send_weights(g)

    def rows_of(mb, c):
        main = tok[mb, :, :, :, block_cols(c)].reshape(256, BLK)
        extra = dot(unpack_extra(c), tok_extra[mb].reshape(128, BLK)).astype(BF16)
        return jnp.concatenate([main, extra], axis=0)

    for copy in local:
        copy.wait()
    from_down.wait_recv()
    acc_a[...] = jnp.zeros_like(acc_a)
    xd[BWD, NG].wait_recv()
    for g in range(NG):
        xd[BWD, g].wait_recv()
        for c in range(*GROUPS[g]):
            acc_a[...] += dot_t(rows_of(BWD, c), dw[:, block_cols(c)])
    from_saved.wait_recv()
    row, col = iota((272, 544), 0), iota((272, 544), 1)
    late = row >= 256
    source = jnp.where(late, (row - 256) >> 1, row >> 5)
    slot = jnp.where(late, 32 + (row & 1), row & 31)
    holder = (source & 3) * 4 + jnp.where(source >= 4, x_t, x)
    chooser = (((col >> 4) == slot) & ((col & 15) == holder)).astype(BF16)
    for h in range(2):
        for kind in range(2):
            sv_rows[kind, :, h * UNITS:(h + 1) * UNITS] = dot(chooser, sv[h, kind].reshape(544, UNITS))

    for h in range(2):
        lanes = pl.ds(h * UNITS, UNITS)
        g_pre, u_pre = sv_rows[0, :, lanes], sv_rows[1, :, lanes]
        sig = jax.nn.sigmoid(g_pre)
        grad = acc_a[:, lanes]
        act_a[:, lanes] = (grad * u_pre * sig * (1.0 + g_pre * (1.0 - sig))).astype(BF16)
        act_b[:, lanes] = (grad * g_pre * sig).astype(BF16)

    xc, zc = {}, {}

    def keep(mb, c, value):
        own[:, block_cols(c)] = value[:128]
        xs[mb, :, :, block_cols(c)] = value[128:256].astype(BF16).reshape(4, 32, BLK)
        own_extra[...] += dot(pack_extra(c), value[256:].astype(BF16))

    def send_part(mb, g):
        if g == NG:
            xs_extra[mb] = own_extra[64:].astype(BF16).reshape(4, 16, BLK)
            src, dst = xs_extra.at[mb], xr_extra.at[mb]
        else:
            src, dst = xs.at[mb, :, :, group_cols(g)], xr.at[mb, :, :, group_cols(g)]
        xc[mb, g] = remote(src, dst, xc_send.at[mb, g], xc_recv.at[mb, g], token_peer)

    def send_sum(mb, g):
        section = after if mb == FWD else before
        xc[mb, g].wait_recv()
        if g == NG:
            zs_extra[mb] = (own_extra[:64].reshape(4, 16, BLK) + xr_extra[mb].astype(F32)).astype(BF16)
        else:
            for c in range(*GROUPS[g]):
                cols = block_cols(c)
                zs[mb, :, :, cols] = (
                    own[:, cols].reshape(4, 32, BLK) + xr[mb, :, :, cols].astype(F32)
                ).astype(BF16)
        for dz in (2, 1, 3, 0):
            tz = (z + dz) % 4
            if g == NG:
                src, dst = zs_extra.at[mb, tz], zr_extra.at[mb, z]
            else:
                src, dst = zs.at[mb, tz, :, group_cols(g)], zr.at[mb, z, :, group_cols(g)]
            zc[mb, g, dz] = remote(
                src, dst, zc_send.at[mb, g, dz], zc_recv.at[mb, g, dz], (section, tz * 4 + x))

    own_extra[...] = jnp.zeros_like(own_extra)
    for g in range(NG):
        from_gate[g].wait_recv()
        from_up[g].wait_recv()
        for c in range(*GROUPS[g]):
            rows = block_cols(c)
            keep(BWD, c, dot_t(act_a[...], gw[rows]) + dot_t(act_b[...], uw[rows]))
        if g + W_AHEAD < NG:
            send_weights(g + W_AHEAD)
        send_part(BWD, g)
        if g == 0:
            pass_rows(FWD, NG)
        pass_rows(FWD, g)
        if g > 0:
            send_sum(BWD, g - 1)
    send_part(BWD, NG)
    send_sum(BWD, NG - 1)
    send_sum(BWD, NG)

    acc_a[...] = jnp.zeros_like(acc_a)
    acc_b[...] = jnp.zeros_like(acc_b)
    xd[FWD, NG].wait_recv()
    for g in range(NG):
        xd[FWD, g].wait_recv()
        for c in range(*GROUPS[g]):
            rows = rows_of(FWD, c)
            acc_a[...] += dot(rows, gw[block_cols(c)])
            acc_b[...] += dot(rows, uw[block_cols(c)])
    act_a[...] = (jax.nn.silu(acc_a[...]) * acc_b[...]).astype(BF16)
    own_extra[...] = jnp.zeros_like(own_extra)
    for g in range(NG):
        for c in range(*GROUPS[g]):
            keep(FWD, c, dot(act_a[...], dw[:, block_cols(c)]))
        send_part(FWD, g)
        if g > 0:
            send_sum(FWD, g - 1)
    send_part(FWD, NG)
    send_sum(FWD, NG - 1)
    send_sum(FWD, NG)

    def place(mb, out):
        infos[mb].wait_recv()
        info = info_r[mb]
        index = info[:, 0:1]
        col = iota((TOK, 128), 1)
        whole = (index == ((col >> 6) * CAP + (col & 31)).astype(F32)).astype(BF16)
        col = iota((TOK, TOK), 1)
        extra_id = (col >> 5) * CAP + 32 + (col & 1)
        for g in (NG, *range(NG)):
            for dz in range(4):
                zc[mb, g, dz].wait_recv()
            if g == NG:
                continue
            for c in range(*GROUPS[g]):
                wanted = jnp.where(((col & 15) >> 1) == c, extra_id, -1).astype(F32)
                value = dot(whole, zr[mb, :, :, block_cols(c)].reshape(128, BLK))
                value += dot((index == wanted).astype(BF16), zr_extra[mb].reshape(64, BLK))
                if mb == FWD:
                    value = info[:, 1:2] * value
                out[0, :, block_cols(c)] = value.astype(BF16)

    place(BWD, out_b)
    place(FWD, out_f)
    for copy in sends:
        copy.wait_send()


def per_device(fi, fr, fw, bg, br, bw, saved, gate, up, down):
    vmem = pl.BlockSpec(memory_space=pltpu.VMEM)
    hbm = pl.BlockSpec(memory_space=pltpu.HBM)
    dma = pltpu.SemaphoreType.DMA
    rows_out = jax.ShapeDtypeStruct((1, TOK, D), BF16)
    saved = saved[0].transpose(0, 2, 1, 3)
    fr, br = fr.reshape(1, TOK), br.reshape(1, TOK)
    return pl.pallas_call(
        kernel,
        out_shape=(rows_out, rows_out),
        in_specs=[hbm] * 10,
        out_specs=(vmem, vmem),
        scratch_shapes=[
            pltpu.VMEM((1, TOK, D), BF16),
            pltpu.VMEM((1, TOK), jnp.int32),
            pltpu.VMEM((1, TOK), F32),
            pltpu.VMEM((1, TOK, D), BF16),
            pltpu.VMEM((1, TOK), jnp.int32),
            pltpu.VMEM((1, TOK), F32),
            pltpu.VMEM((D, 2 * UNITS), BF16),
            pltpu.VMEM((D, 2 * UNITS), BF16),
            pltpu.VMEM((2 * UNITS, D), BF16),
            pltpu.VMEM((2, 2, CAP, 16, UNITS), BF16),
            pltpu.VMEM((2, 272, 256), F32),
            pltpu.VMEM((2, 2, 32, D), BF16),
            pltpu.VMEM((2, 2, 16, BLK), BF16),
            pltpu.VMEM((2, 2, 4, 32, D), BF16),
            pltpu.VMEM((2, 2, 4, 16, BLK), BF16),
            pltpu.VMEM((2, TOK, 128), F32),
            pltpu.VMEM((2, TOK, 128), F32),
            pltpu.VMEM((272, 256), F32),
            pltpu.VMEM((272, 256), F32),
            pltpu.VMEM((272, 256), BF16),
            pltpu.VMEM((272, 256), BF16),
            pltpu.VMEM((128, D), F32),
            pltpu.VMEM((128, BLK), F32),
            pltpu.VMEM((2, 4, 32, D), BF16),
            pltpu.VMEM((2, 4, 16, BLK), BF16),
            pltpu.VMEM((2, 4, 32, D), BF16),
            pltpu.VMEM((2, 4, 16, BLK), BF16),
            pltpu.VMEM((2, 4, 32, D), BF16),
            pltpu.VMEM((2, 4, 16, BLK), BF16),
            pltpu.VMEM((2, 4, 32, D), BF16),
            pltpu.VMEM((2, 4, 16, BLK), BF16),
            dma((10,)),
            dma((2 + 2 * NG,)),
            dma((2 + 2 * NG,)),
            dma((2,)),
            dma((2,)),
            dma((2, NG + 1, 3)),
            dma((2, NG + 1, 3)),
            dma((2, NG + 1)),
            dma((2, NG + 1)),
            dma((2, NG + 1)),
            dma((2, NG + 1)),
            dma((2, NG + 1, 4)),
            dma((2, NG + 1, 4)),
        ],
        compiler_params=pltpu.CompilerParams(
            collective_id=0, has_side_effects=True, vmem_limit_bytes=60 * 2**20
        ),
        name="routed_experts",
    )(fi, fr, fw, bg, br, bw, saved, gate, up, down)


def solution(mesh):
    placed = (
        P("pipe", "expert", None),
        P("pipe", "expert", None),
        P("pipe", "expert"),
        P("pipe", "expert", None),
        P("pipe", "expert", None),
        P("pipe", "expert"),
        P("pipe", None, None, None, "expert"),
        P("pipe", None, "expert"),
        P("pipe", None, "expert"),
        P("pipe", "expert", None),
    )
    return jax.shard_map(
        per_device,
        mesh=mesh,
        in_specs=placed,
        out_specs=(P("pipe", "expert", None), P("pipe", "expert", None)),
        check_vma=False,
    )
```

```python
import jax
import jax.numpy as jnp
from jax import lax
from jax.experimental import pallas as pl
from jax.experimental.pallas import tpu as pltpu
from jax.sharding import PartitionSpec as P

MESH = pl.DeviceIdType.MESH
BF16 = jnp.bfloat16
F32 = jnp.float32
CAP = 34
TOK = 64
D = 3584
UNITS = 128
BLK = 512
NBLK = D // BLK
HALF = BLK // 2
WIDE = D + HALF
TAIL = pl.ds(D, HALF)
GROUPS = ((0, 2), (2, 4), (4, 6), (6, 7))
NG = len(GROUPS)
FWD, BWD = 0, 1
STEPS = (0, 2, 1, 3)
W_FIRST = 2
W_AHEAD = 4
B_LAG = 2
F_OWN_EARLY = True


def iota(shape, dim):
    return lax.broadcasted_iota(jnp.int32, shape, dim)


def dot(a, b):
    return jnp.dot(a, b, preferred_element_type=F32)


def dot_t(a, b):
    return lax.dot_general(a, b, (((1,), (1,)), ((), ())), preferred_element_type=F32)


def group_cols(g):
    first, last = GROUPS[g]
    return pl.ds(first * BLK, (last - first) * BLK)


def message_cols(g):
    first, last = GROUPS[g]
    return pl.ds(first * BLK, (last - first) * BLK + (HALF if g == NG - 1 else 0))


def block_cols(c):
    return pl.ds(c * BLK, BLK)


def column(values):
    diagonal = iota((TOK, TOK), 0) == iota((TOK, TOK), 1)
    spread = jnp.where(diagonal, jnp.broadcast_to(values.astype(F32), (TOK, TOK)), 0.0)
    return jnp.broadcast_to(jnp.sum(spread, axis=1, keepdims=True), (TOK, 128))


def row_index(route):
    to_one = (route == 1).astype(F32)
    earlier = (iota((TOK, TOK), 1) < iota((TOK, TOK), 0)).astype(BF16)
    ones_before = dot(earlier, to_one.astype(BF16))
    place = iota((TOK, 128), 0).astype(F32)
    return jnp.where(route == 1, CAP + ones_before, place - ones_before)


def tokens_in_lanes(index):
    diagonal = iota((TOK, TOK), 0) == iota((TOK, TOK), 1)
    spread = jnp.where(diagonal, index[:, :TOK], 0.0).astype(BF16)
    return dot(jnp.ones((TOK, TOK), BF16), spread)


def extra_match(short, long, c, half):
    if half is None:
        source = short >> 1
    else:
        source = jnp.where(short < 8, ((short >> 2) << 2) + 2 * half + ((short >> 1) & 1), -1)
    return (((long >> 4) == source) & ((long & 15) == 2 * c + (short & 1))).astype(BF16)


def unpack_extra(c, packed):
    short, long = iota((16, packed.shape[0]), 0), iota((16, packed.shape[0]), 1)
    source = short >> 1
    place = 2 * c + (short & 1)
    parts = [
        dot((((long >> 5) == source) & ((long & 31) == place + up)).astype(BF16), packed)
        for up in (0, 16)
    ]
    return jnp.concatenate(parts, axis=1).astype(BF16)


def pack_extra(c, half):
    return extra_match(iota((128, 16), 1), iota((128, 16), 0), c, half)


def kernel(
    fi_in, fr_in, fw_in, bg_in, br_in, bw_in, saved, gate, up, down,
    out_f, out_b,
    fi, fr, fw, bg, br, bw,
    gw, uw, dw, sv, sv_rows, sv_send,
    ds_main, tok,
    info_s, info_r,
    acc_a, acc_b, act_a, act_b,
    own, own_extra,
    xs, xr, zs, zr,
    loc_sem,
    w_send, w_recv, i_send, i_recv,
    zd_send, zd_recv, xd_send, xd_recv,
    xc_send, xc_recv, zc_send, zc_recv,
):
    p = lax.axis_index("pipe")
    e = lax.axis_index("expert")
    z, x = e // 4, e % 4
    turn = 1 - 2 * ((x + p) % 2)
    x_w = (x + turn + 4) % 4
    x_t = (x - turn + 4) % 4
    weight_peer = (p, z * 4 + x_w)
    token_peer = (p, z * 4 + x_t)
    after, before = (p + 1) % 16, (p + 15) % 16

    barrier = pltpu.get_barrier_semaphore()
    peers = [weight_peer, token_peer]
    peers += [(p, ((z + dz) % 4) * 4 + x) for dz in range(1, 4)]
    peers += [(q, ((z + dz) % 4) * 4 + x) for q in (after, before) for dz in range(4)]
    for peer in peers:
        pl.semaphore_signal(barrier, inc=1, device_id=peer, device_id_type=MESH)

    sends = []

    def remote(src, dst, send, recv, peer):
        copy = pltpu.make_async_remote_copy(
            src_ref=src, dst_ref=dst, send_sem=send, recv_sem=recv,
            device_id=peer, device_id_type=MESH,
        )
        copy.start()
        sends.append(copy)
        return copy

    small = [
        pltpu.make_async_copy(src, dst, loc_sem.at[4 + i])
        for i, (src, dst) in enumerate(
            ((br_in, br), (bw_in, bw), (bg_in, bg), (fr_in, fr), (fw_in, fw), (fi_in, fi))
        )
    ]
    for copy in small:
        copy.start()
    local = [
        pltpu.make_async_copy(gate.at[0], gw.at[:, pl.ds(0, UNITS)], loc_sem.at[0]),
        pltpu.make_async_copy(up.at[0], uw.at[:, pl.ds(0, UNITS)], loc_sem.at[1]),
        pltpu.make_async_copy(down.at[0], dw.at[pl.ds(0, UNITS)], loc_sem.at[2]),
        pltpu.make_async_copy(saved, sv, loc_sem.at[3]),
    ]
    for copy in local:
        copy.start()

    def read_grad(c):
        return (grad_col[:, :1] * bg[0, :, block_cols(c)].astype(F32)).astype(BF16)

    def read_input(c):
        return fi[0, :, block_cols(c)]

    def pick_main(mb, by_lane, read, g):
        row = iota((TOK, TOK), 0)
        picker = (by_lane == ((row >> 5) * CAP + (row & 31)).astype(F32)).astype(BF16)
        for c in range(*GROUPS[g]):
            picked = dot(picker, read(c)).astype(BF16)
            ds_main[mb, 0, :, block_cols(c)] = picked[:32]
            ds_main[mb, 1, :, block_cols(c)] = picked[32:]

    def pick_extra(mb, by_lane, read):
        row = iota((32, TOK), 0)
        extra_id = (row >> 4) * CAP + 32 + (row & 1)
        extra = jnp.zeros((32, BLK), F32)
        for c in range(NBLK):
            wanted = jnp.where(((row & 15) >> 1) == c, extra_id, -1).astype(F32)
            extra += dot((by_lane[:32] == wanted).astype(BF16), read(c))
        extra = extra.astype(BF16)
        for k in range(2):
            ds_main[mb, k, 0:16, TAIL] = extra[16 * k:16 * k + 16, :HALF]
            ds_main[mb, k, 16:32, TAIL] = extra[16 * k:16 * k + 16, HALF:]
        tok[mb, 0, 0] = ds_main[mb, z // 2]

    zd = {}
    xd = {}

    def send_rows(mb, at):
        tz = (z + STEPS[at]) % 4
        zd[mb, at] = remote(
            ds_main.at[mb, tz // 2], tok.at[mb, 0, at],
            zd_send.at[mb, at - 1], zd_recv.at[mb, at - 1], (p, tz * 4 + x))

    def pass_rows(mb, at):
        if at > 0:
            zd[mb, at].wait_recv()
        xd[mb, at] = remote(
            tok.at[mb, 0, at], tok.at[mb, 1, at], xd_send.at[mb, at], xd_recv.at[mb, at], token_peer)

    def wait_rows(mb, at):
        xd[mb, at].wait_recv()

    from_gate, from_up = [], []

    def send_weights(g):
        cols = group_cols(g)
        from_gate.append(remote(
            gate.at[0, cols], gw.at[cols, pl.ds(UNITS, UNITS)],
            w_send.at[2 + g], w_recv.at[2 + g], weight_peer))
        from_up.append(remote(
            up.at[0, cols], uw.at[cols, pl.ds(UNITS, UNITS)],
            w_send.at[2 + NG + g], w_recv.at[2 + NG + g], weight_peer))

    pl.semaphore_wait(barrier, len(peers))
    from_down = remote(down.at[0], dw.at[pl.ds(UNITS, UNITS)], w_send.at[0], w_recv.at[0], weight_peer)
    for copy in small[:3]:
        copy.wait()
    index_b = row_index(column(br[...]))
    grad_col = column(bw[...])
    info_s[BWD] = index_b
    lanes_b = tokens_in_lanes(index_b)
    for g in range(NG):
        pick_main(BWD, lanes_b, read_grad, g)
    pick_extra(BWD, lanes_b, read_grad)
    for at in range(1, 4):
        send_rows(BWD, at)
    pass_rows(BWD, 0)

    for copy in local:
        copy.wait()
    row, col = iota((272, 544), 0), iota((272, 544), 1)
    late = row >= 256
    source = jnp.where(late, (row - 256) >> 1, row >> 5)
    slot = jnp.where(late, 32 + (row & 1), row & 31)
    step = ((source & 1) << 1) | ((source >> 1) & 1)
    holder = ((z + 4 - step) & 3) * 4
    in_slot = (col >> 4) == slot
    mine = holder + jnp.where(source >= 4, x_t, x) == (col & 15)
    theirs = holder + jnp.where(source >= 4, (x + 2) % 4, x_w) == (col & 15)
    for kind in range(2):
        stored = sv[kind].reshape(544, UNITS)
        sv_send[kind] = dot((in_slot & theirs).astype(BF16), stored).astype(BF16)
        sv_rows[kind, :, 0:UNITS] = dot((in_slot & mine).astype(BF16), stored).astype(BF16)
    from_saved = remote(
        sv_send, sv_rows.at[:, :, pl.ds(UNITS, UNITS)], w_send.at[1], w_recv.at[1], weight_peer)

    for copy in small[3:]:
        copy.wait()
    index_f = row_index(column(fr[...]))
    info_s[FWD] = jnp.where(iota((TOK, 128), 1) == 1, column(fw[...]), index_f)
    lanes_f = tokens_in_lanes(index_f)
    infos = [
        remote(info_s.at[FWD], info_r.at[FWD], i_send.at[FWD], i_recv.at[FWD], (after, e)),
        remote(info_s.at[BWD], info_r.at[BWD], i_send.at[BWD], i_recv.at[BWD], (before, e)),
    ]
    for g in range(NG):
        pick_main(FWD, lanes_f, read_input, g)
    pick_extra(FWD, lanes_f, read_input)

    for g in range(W_FIRST):
        send_weights(g)
    if F_OWN_EARLY:
        pass_rows(FWD, 0)
    pass_rows(BWD, 2)
    send_rows(FWD, 1)
    pass_rows(BWD, 3)
    send_rows(FWD, 2)
    send_rows(FWD, 3)
    pass_rows(BWD, 1)
    for g in range(W_FIRST, W_AHEAD):
        send_weights(g)

    def rows_of(mb, c, half):
        count = 4 if half is None else 2
        first = 2 * half if half else 0
        main = tok[mb, :, first:first + count, :, block_cols(c)].reshape(64 * count, BLK)
        packed = tok[mb, :, first:first + count, :, TAIL].reshape(64 * count, HALF)
        extra = unpack_extra(c, packed)
        return jnp.concatenate([main, extra], axis=0)

    from_down.wait_recv()
    acc_a[...] = jnp.zeros_like(acc_a)
    for at in range(4):
        wait_rows(BWD, at)
    for c in range(NBLK):
        acc_a[...] += dot_t(rows_of(BWD, c, None), dw[:, block_cols(c)])
    from_saved.wait_recv()
    for h in range(2):
        lanes = pl.ds(h * UNITS, UNITS)
        g_pre, u_pre = sv_rows[0, :, lanes].astype(F32), sv_rows[1, :, lanes].astype(F32)
        sig = jax.nn.sigmoid(g_pre)
        grad = acc_a[:, lanes]
        act_a[:, lanes] = (grad * u_pre * sig * (1.0 + g_pre * (1.0 - sig))).astype(BF16)
        act_b[:, lanes] = (grad * g_pre * sig).astype(BF16)

    xc, zc = {}, {}

    def span(half):
        return (0, 4) if half is None else (2 * half, 2)

    def keep(mb, c, value, half):
        first, count = span(half)
        rows = 32 * count
        own[32 * first:32 * first + rows, block_cols(c)] = value[:rows]
        xs[mb, first:first + count, :, block_cols(c)] = (
            value[rows:2 * rows].astype(BF16).reshape(count, 32, BLK))
        own_extra[...] += dot(pack_extra(c, half), value[2 * rows:].astype(BF16))

    def send_part(mb, g, half):
        first, count = span(half)
        some = pl.ds(first, count)
        if g == NG - 1:
            packed = own_extra[64 + 16 * first:64 + 16 * (first + count)].astype(BF16).reshape(count, 16, BLK)
            xs[mb, first:first + count, 0:16, TAIL] = packed[:, :, :HALF]
            xs[mb, first:first + count, 16:32, TAIL] = packed[:, :, HALF:]
        src, dst = xs.at[mb, some, :, message_cols(g)], xr.at[mb, some, :, message_cols(g)]
        h = half or 0
        xc[mb, g, h] = remote(src, dst, xc_send.at[mb, h, g], xc_recv.at[mb, h, g], token_peer)

    def send_sum(mb, g, half):
        section = after if mb == FWD else before
        first, count = span(half)
        xc[mb, g, half or 0].wait_recv()
        if g == NG - 1:
            packed = own_extra[16 * first:16 * (first + count)].reshape(count, 16, BLK)
            for top, lanes in ((0, slice(0, HALF)), (16, slice(HALF, BLK))):
                zs[mb, first:first + count, top:top + 16, TAIL] = (
                    packed[:, :, lanes] + xr[mb, first:first + count, top:top + 16, TAIL].astype(F32)
                ).astype(BF16)
        for c in range(*GROUPS[g]):
            cols = block_cols(c)
            zs[mb, first:first + count, :, cols] = (
                own[32 * first:32 * (first + count), cols].reshape(count, 32, BLK)
                + xr[mb, first:first + count, :, cols].astype(F32)
            ).astype(BF16)
        for at in (1, 2, 3, 0):
            if not first <= at < first + count:
                continue
            tz = (z + 4 - STEPS[at]) % 4
            src, dst = zs.at[mb, at, :, message_cols(g)], zr.at[mb, at, :, message_cols(g)]
            zc[mb, g, at] = remote(
                src, dst, zc_send.at[mb, g, at], zc_recv.at[mb, g, at], (section, tz * 4 + x))

    own_extra[...] = jnp.zeros_like(own_extra)
    for g in range(NG):
        from_gate[g].wait_recv()
        from_up[g].wait_recv()
        for c in range(*GROUPS[g]):
            rows = block_cols(c)
            keep(BWD, c, dot_t(act_a[...], gw[rows]) + dot_t(act_b[...], uw[rows]), None)
        if g + W_AHEAD < NG:
            send_weights(g + W_AHEAD)
        send_part(BWD, g, None)
        if g >= B_LAG:
            send_sum(BWD, g - B_LAG, None)
    if not F_OWN_EARLY:
        pass_rows(FWD, 0)
    pass_rows(FWD, 1)
    for g in range(max(NG - B_LAG, 0), NG):
        send_sum(BWD, g, None)
    pass_rows(FWD, 2)
    pass_rows(FWD, 3)

    for half in range(2):
        for at in (2 * half, 2 * half + 1):
            wait_rows(FWD, at)
        acc_a[:144] = jnp.zeros((144, 256), F32)
        acc_b[:144] = jnp.zeros((144, 256), F32)
        for c in range(NBLK):
            rows = rows_of(FWD, c, half)
            acc_a[:144] += dot(rows, gw[block_cols(c)])
            acc_b[:144] += dot(rows, uw[block_cols(c)])
        act_a[:144] = (jax.nn.silu(acc_a[:144]) * acc_b[:144]).astype(BF16)
        own_extra[...] = jnp.zeros_like(own_extra)
        for g in range(NG):
            for c in range(*GROUPS[g]):
                keep(FWD, c, dot(act_a[:144], dw[:, block_cols(c)]), half)
            send_part(FWD, g, half)
        for g in range(NG):
            send_sum(FWD, g, half)

    def place(mb, out):
        infos[mb].wait_recv()
        info = info_r[mb]
        index = info[:, 0:1]
        def first_row(at):
            step = ((at & 1) << 1) | (at >> 1)
            return (((z + step) & 3) >> 1) * CAP

        col = iota((TOK, 128), 1)
        whole = (index == (first_row(col >> 5) + (col & 31)).astype(F32)).astype(BF16)
        extra_id = first_row(col >> 5) + 32 + (col & 1)
        for g in range(NG):
            for at in range(4):
                zc[mb, g, at].wait_recv()
        packed = zr[mb, :, :, TAIL].reshape(128, HALF)
        for c in range(NBLK):
            value = dot(whole, zr[mb, :, :, block_cols(c)].reshape(128, BLK))
            extra = []
            for up in (0, 8):
                wanted = jnp.where(((col & 31) >> 1) == c + up, extra_id, -1).astype(F32)
                extra.append(dot((index == wanted).astype(BF16), packed))
            value += jnp.concatenate(extra, axis=1)
            if mb == FWD:
                value = info[:, 1:2] * value
            out[0, :, block_cols(c)] = value.astype(BF16)

    place(BWD, out_b)
    place(FWD, out_f)
    for copy in sends:
        copy.wait_send()


def per_device(fi, fr, fw, bg, br, bw, saved, gate, up, down):
    vmem = pl.BlockSpec(memory_space=pltpu.VMEM)
    hbm = pl.BlockSpec(memory_space=pltpu.HBM)
    dma = pltpu.SemaphoreType.DMA
    rows_out = jax.ShapeDtypeStruct((1, TOK, D), BF16)
    saved = saved[0].transpose(0, 2, 1, 3)
    fr, br = fr.reshape(1, TOK), br.reshape(1, TOK)
    return pl.pallas_call(
        kernel,
        out_shape=(rows_out, rows_out),
        in_specs=[hbm] * 10,
        out_specs=(vmem, vmem),
        scratch_shapes=[
            pltpu.VMEM((1, TOK, D), BF16),
            pltpu.VMEM((1, TOK), jnp.int32),
            pltpu.VMEM((1, TOK), F32),
            pltpu.VMEM((1, TOK, D), BF16),
            pltpu.VMEM((1, TOK), jnp.int32),
            pltpu.VMEM((1, TOK), F32),
            pltpu.VMEM((D, 2 * UNITS), BF16),
            pltpu.VMEM((D, 2 * UNITS), BF16),
            pltpu.VMEM((2 * UNITS, D), BF16),
            pltpu.VMEM((2, CAP, 16, UNITS), BF16),
            pltpu.VMEM((2, 272, 256), BF16),
            pltpu.VMEM((2, 272, UNITS), BF16),
            pltpu.VMEM((2, 2, 32, WIDE), BF16),
            pltpu.VMEM((2, 2, 4, 32, WIDE), BF16),
            pltpu.VMEM((2, TOK, 128), F32),
            pltpu.VMEM((2, TOK, 128), F32),
            pltpu.VMEM((272, 256), F32),
            pltpu.VMEM((272, 256), F32),
            pltpu.VMEM((272, 256), BF16),
            pltpu.VMEM((272, 256), BF16),
            pltpu.VMEM((128, D), F32),
            pltpu.VMEM((128, BLK), F32),
            pltpu.VMEM((2, 4, 32, WIDE), BF16),
            pltpu.VMEM((2, 4, 32, WIDE), BF16),
            pltpu.VMEM((2, 4, 32, WIDE), BF16),
            pltpu.VMEM((2, 4, 32, WIDE), BF16),
            dma((10,)),
            dma((2 + 2 * NG,)),
            dma((2 + 2 * NG,)),
            dma((2,)),
            dma((2,)),
            dma((2, 3)),
            dma((2, 3)),
            dma((2, 4)),
            dma((2, 4)),
            dma((2, 2, NG)),
            dma((2, 2, NG)),
            dma((2, NG, 4)),
            dma((2, NG, 4)),
        ],
        compiler_params=pltpu.CompilerParams(
            collective_id=0, has_side_effects=True, vmem_limit_bytes=60 * 2**20
        ),
        name="routed_experts",
    )(fi, fr, fw, bg, br, bw, saved, gate, up, down)


def solution(mesh):
    placed = (
        P("pipe", "expert", None),
        P("pipe", "expert", None),
        P("pipe", "expert"),
        P("pipe", "expert", None),
        P("pipe", "expert", None),
        P("pipe", "expert"),
        P("pipe", None, None, None, "expert"),
        P("pipe", None, "expert"),
        P("pipe", None, "expert"),
        P("pipe", "expert", None),
    )
    return jax.shard_map(
        per_device,
        mesh=mesh,
        in_specs=placed,
        out_specs=(P("pipe", "expert", None), P("pipe", "expert", None)),
        check_vma=False,
    )
```

```python
import jax
import jax.numpy as jnp
from jax import lax
from jax.experimental import pallas as pl
from jax.experimental.pallas import tpu as pltpu
from jax.sharding import PartitionSpec as P

MESH = pl.DeviceIdType.MESH
BF16 = jnp.bfloat16
F32 = jnp.float32
CAP = 34
TOK = 64
D = 3584
UNITS = 128
BLK = 512
NBLK = D // BLK
HALF = BLK // 2
WIDE = D + HALF
TAIL = pl.ds(D, HALF)
GROUPS = ((0, 1), (1, 3), (3, 5), (5, 6), (6, 7))
NG = len(GROUPS)
FWD, BWD = 0, 1
STEPS = (0, 2, 1, 3)
W_FIRST = 2
W_AHEAD = 5
B_LAG = 2
F_OWN_EARLY = True


def iota(shape, dim):
    return lax.broadcasted_iota(jnp.int32, shape, dim)


def dot(a, b):
    return jnp.dot(a, b, preferred_element_type=F32)


def dot_t(a, b):
    return lax.dot_general(a, b, (((1,), (1,)), ((), ())), preferred_element_type=F32)


def group_cols(g):
    first, last = GROUPS[g]
    return pl.ds(first * BLK, (last - first) * BLK)


def message_cols(g):
    first, last = GROUPS[g]
    return pl.ds(first * BLK, (last - first) * BLK + (HALF if g == NG - 1 else 0))


def block_cols(c):
    return pl.ds(c * BLK, BLK)


def column(values):
    diagonal = iota((TOK, TOK), 0) == iota((TOK, TOK), 1)
    spread = jnp.where(diagonal, jnp.broadcast_to(values.astype(F32), (TOK, TOK)), 0.0)
    return jnp.broadcast_to(jnp.sum(spread, axis=1, keepdims=True), (TOK, 128))


def row_index(route):
    to_one = (route == 1).astype(F32)
    earlier = (iota((TOK, TOK), 1) < iota((TOK, TOK), 0)).astype(BF16)
    ones_before = dot(earlier, to_one.astype(BF16))
    place = iota((TOK, 128), 0).astype(F32)
    return jnp.where(route == 1, CAP + ones_before, place - ones_before)


def tokens_in_lanes(index):
    diagonal = iota((TOK, TOK), 0) == iota((TOK, TOK), 1)
    spread = jnp.where(diagonal, index[:, :TOK], 0.0).astype(BF16)
    return dot(jnp.ones((TOK, TOK), BF16), spread)


def extra_match(short, long, c, half):
    if half is None:
        source = short >> 1
    else:
        source = jnp.where(short < 8, ((short >> 2) << 2) + 2 * half + ((short >> 1) & 1), -1)
    return (((long >> 4) == source) & ((long & 15) == 2 * c + (short & 1))).astype(BF16)


def unpack_extra(c, packed):
    short, long = iota((16, packed.shape[0]), 0), iota((16, packed.shape[0]), 1)
    source = short >> 1
    place = 2 * c + (short & 1)
    parts = [
        dot((((long >> 5) == source) & ((long & 31) == place + up)).astype(BF16), packed)
        for up in (0, 16)
    ]
    return jnp.concatenate(parts, axis=1).astype(BF16)


def pack_extra(c, half):
    return extra_match(iota((128, 16), 1), iota((128, 16), 0), c, half)


def kernel(
    fi_in, fr_in, fw_in, bg_in, br_in, bw_in, saved, gate, up, down,
    out_f, out_b,
    fi, fr, fw, bg, br, bw,
    gw, uw, dw, sv, sv_rows, sv_send,
    ds_main, tok,
    info_s, info_r,
    acc_a, acc_b, act_a, act_b,
    own, own_extra,
    xs, xr, zs, zr,
    loc_sem,
    w_send, w_recv, i_send, i_recv,
    zd_send, zd_recv, xd_send, xd_recv,
    xc_send, xc_recv, zc_send, zc_recv,
):
    p = lax.axis_index("pipe")
    e = lax.axis_index("expert")
    z, x = e // 4, e % 4
    turn = 1 - 2 * ((x + p) % 2)
    x_w = (x + turn + 4) % 4
    x_t = (x - turn + 4) % 4
    weight_peer = (p, z * 4 + x_w)
    token_peer = (p, z * 4 + x_t)
    after, before = (p + 1) % 16, (p + 15) % 16

    barrier = pltpu.get_barrier_semaphore()
    peers = [weight_peer, token_peer]
    peers += [(p, ((z + dz) % 4) * 4 + x) for dz in range(1, 4)]
    peers += [(q, ((z + dz) % 4) * 4 + x) for q in (after, before) for dz in range(4)]
    for peer in peers:
        pl.semaphore_signal(barrier, inc=1, device_id=peer, device_id_type=MESH)

    sends = []

    def remote(src, dst, send, recv, peer):
        copy = pltpu.make_async_remote_copy(
            src_ref=src, dst_ref=dst, send_sem=send, recv_sem=recv,
            device_id=peer, device_id_type=MESH,
        )
        copy.start()
        sends.append(copy)
        return copy

    small = [
        pltpu.make_async_copy(src, dst, loc_sem.at[4 + i])
        for i, (src, dst) in enumerate(
            ((br_in, br), (bw_in, bw), (bg_in, bg), (fr_in, fr), (fw_in, fw), (fi_in, fi))
        )
    ]
    for copy in small:
        copy.start()
    local = [
        pltpu.make_async_copy(gate.at[0], gw.at[:, pl.ds(0, UNITS)], loc_sem.at[0]),
        pltpu.make_async_copy(up.at[0], uw.at[:, pl.ds(0, UNITS)], loc_sem.at[1]),
        pltpu.make_async_copy(down.at[0], dw.at[pl.ds(0, UNITS)], loc_sem.at[2]),
        pltpu.make_async_copy(saved, sv, loc_sem.at[3]),
    ]
    for copy in local:
        copy.start()

    def read_grad(c):
        return (grad_col[:, :1] * bg[0, :, block_cols(c)].astype(F32)).astype(BF16)

    def read_input(c):
        return fi[0, :, block_cols(c)]

    def pick_main(mb, by_lane, read, g):
        row = iota((TOK, TOK), 0)
        picker = (by_lane == ((row >> 5) * CAP + (row & 31)).astype(F32)).astype(BF16)
        for c in range(*GROUPS[g]):
            picked = dot(picker, read(c)).astype(BF16)
            ds_main[mb, 0, :, block_cols(c)] = picked[:32]
            ds_main[mb, 1, :, block_cols(c)] = picked[32:]

    def pick_extra(mb, by_lane, read):
        row = iota((32, TOK), 0)
        extra_id = (row >> 4) * CAP + 32 + (row & 1)
        extra = jnp.zeros((32, BLK), F32)
        for c in range(NBLK):
            wanted = jnp.where(((row & 15) >> 1) == c, extra_id, -1).astype(F32)
            extra += dot((by_lane[:32] == wanted).astype(BF16), read(c))
        extra = extra.astype(BF16)
        for k in range(2):
            ds_main[mb, k, 0:16, TAIL] = extra[16 * k:16 * k + 16, :HALF]
            ds_main[mb, k, 16:32, TAIL] = extra[16 * k:16 * k + 16, HALF:]
        tok[mb, 0, 0] = ds_main[mb, z // 2]

    zd = {}
    xd = {}

    def send_rows(mb, at):
        tz = (z + STEPS[at]) % 4
        zd[mb, at] = remote(
            ds_main.at[mb, tz // 2], tok.at[mb, 0, at],
            zd_send.at[mb, at - 1], zd_recv.at[mb, at - 1], (p, tz * 4 + x))

    def pass_rows(mb, at):
        if at > 0:
            zd[mb, at].wait_recv()
        xd[mb, at] = remote(
            tok.at[mb, 0, at], tok.at[mb, 1, at], xd_send.at[mb, at], xd_recv.at[mb, at], token_peer)

    def wait_rows(mb, at):
        xd[mb, at].wait_recv()

    from_gate, from_up = [], []

    def send_weights(g):
        cols = group_cols(g)
        from_gate.append(remote(
            gate.at[0, cols], gw.at[cols, pl.ds(UNITS, UNITS)],
            w_send.at[2 + g], w_recv.at[2 + g], weight_peer))
        from_up.append(remote(
            up.at[0, cols], uw.at[cols, pl.ds(UNITS, UNITS)],
            w_send.at[2 + NG + g], w_recv.at[2 + NG + g], weight_peer))

    for copy in small[:3]:
        copy.wait()
    index_b = row_index(column(br[...]))
    grad_col = column(bw[...])
    info_s[BWD] = index_b
    lanes_b = tokens_in_lanes(index_b)
    for g in range(NG):
        pick_main(BWD, lanes_b, read_grad, g)
    pick_extra(BWD, lanes_b, read_grad)
    pl.semaphore_wait(barrier, len(peers))
    from_down = remote(down.at[0], dw.at[pl.ds(UNITS, UNITS)], w_send.at[0], w_recv.at[0], weight_peer)
    for at in range(1, 4):
        send_rows(BWD, at)
    pass_rows(BWD, 0)

    for copy in local:
        copy.wait()
    row, col = iota((272, 544), 0), iota((272, 544), 1)
    late = row >= 256
    source = jnp.where(late, (row - 256) >> 1, row >> 5)
    slot = jnp.where(late, 32 + (row & 1), row & 31)
    step = ((source & 1) << 1) | ((source >> 1) & 1)
    holder = ((z + 4 - step) & 3) * 4
    in_slot = (col >> 4) == slot
    mine = holder + jnp.where(source >= 4, x_t, x) == (col & 15)
    theirs = holder + jnp.where(source >= 4, (x + 2) % 4, x_w) == (col & 15)
    for kind in range(2):
        stored = sv[kind].reshape(544, UNITS)
        sv_send[kind] = dot((in_slot & theirs).astype(BF16), stored).astype(BF16)
        sv_rows[kind, :, 0:UNITS] = dot((in_slot & mine).astype(BF16), stored).astype(BF16)
    from_saved = remote(
        sv_send, sv_rows.at[:, :, pl.ds(UNITS, UNITS)], w_send.at[1], w_recv.at[1], weight_peer)

    for copy in small[3:]:
        copy.wait()
    index_f = row_index(column(fr[...]))
    info_s[FWD] = jnp.where(iota((TOK, 128), 1) == 1, column(fw[...]), index_f)
    lanes_f = tokens_in_lanes(index_f)
    infos = [
        remote(info_s.at[FWD], info_r.at[FWD], i_send.at[FWD], i_recv.at[FWD], (after, e)),
        remote(info_s.at[BWD], info_r.at[BWD], i_send.at[BWD], i_recv.at[BWD], (before, e)),
    ]
    for g in range(NG):
        pick_main(FWD, lanes_f, read_input, g)
    pick_extra(FWD, lanes_f, read_input)

    for g in range(W_FIRST):
        send_weights(g)
    if F_OWN_EARLY:
        pass_rows(FWD, 0)
    pass_rows(BWD, 2)
    send_rows(FWD, 1)
    pass_rows(BWD, 3)
    send_rows(FWD, 2)
    send_rows(FWD, 3)
    pass_rows(BWD, 1)
    for g in range(W_FIRST, W_AHEAD):
        send_weights(g)

    def rows_of(mb, c, half):
        count = 4 if half is None else 2
        first = 2 * half if half else 0
        main = tok[mb, :, first:first + count, :, block_cols(c)].reshape(64 * count, BLK)
        packed = tok[mb, :, first:first + count, :, TAIL].reshape(64 * count, HALF)
        extra = unpack_extra(c, packed)
        return jnp.concatenate([main, extra], axis=0)

    from_down.wait_recv()
    acc_a[...] = jnp.zeros_like(acc_a)
    for at in range(4):
        wait_rows(BWD, at)
    for c in range(NBLK):
        acc_a[...] += dot_t(rows_of(BWD, c, None), dw[:, block_cols(c)])
    from_saved.wait_recv()
    for h in range(2):
        lanes = pl.ds(h * UNITS, UNITS)
        g_pre, u_pre = sv_rows[0, :, lanes].astype(F32), sv_rows[1, :, lanes].astype(F32)
        sig = jax.nn.sigmoid(g_pre)
        grad = acc_a[:, lanes]
        act_a[:, lanes] = (grad * u_pre * sig * (1.0 + g_pre * (1.0 - sig))).astype(BF16)
        act_b[:, lanes] = (grad * g_pre * sig).astype(BF16)

    xc, zc = {}, {}

    def span(half):
        return (0, 4) if half is None else (2 * half, 2)

    def keep(mb, c, value, half):
        first, count = span(half)
        rows = 32 * count
        own[32 * first:32 * first + rows, block_cols(c)] = value[:rows]
        xs[mb, first:first + count, :, block_cols(c)] = (
            value[rows:2 * rows].astype(BF16).reshape(count, 32, BLK))
        own_extra[...] += dot(pack_extra(c, half), value[2 * rows:].astype(BF16))

    def send_part(mb, g, half):
        first, count = span(half)
        some = pl.ds(first, count)
        if g == NG - 1:
            packed = own_extra[64 + 16 * first:64 + 16 * (first + count)].astype(BF16).reshape(count, 16, BLK)
            xs[mb, first:first + count, 0:16, TAIL] = packed[:, :, :HALF]
            xs[mb, first:first + count, 16:32, TAIL] = packed[:, :, HALF:]
        src, dst = xs.at[mb, some, :, message_cols(g)], xr.at[mb, some, :, message_cols(g)]
        h = half or 0
        xc[mb, g, h] = remote(src, dst, xc_send.at[mb, h, g], xc_recv.at[mb, h, g], token_peer)

    def send_sum(mb, g, half):
        section = after if mb == FWD else before
        first, count = span(half)
        xc[mb, g, half or 0].wait_recv()
        if g == NG - 1:
            packed = own_extra[16 * first:16 * (first + count)].reshape(count, 16, BLK)
            for top, lanes in ((0, slice(0, HALF)), (16, slice(HALF, BLK))):
                zs[mb, first:first + count, top:top + 16, TAIL] = (
                    packed[:, :, lanes] + xr[mb, first:first + count, top:top + 16, TAIL].astype(F32)
                ).astype(BF16)
        for c in range(*GROUPS[g]):
            cols = block_cols(c)
            zs[mb, first:first + count, :, cols] = (
                own[32 * first:32 * (first + count), cols].reshape(count, 32, BLK)
                + xr[mb, first:first + count, :, cols].astype(F32)
            ).astype(BF16)
        for at in (1, 2, 3, 0):
            if not first <= at < first + count:
                continue
            tz = (z + 4 - STEPS[at]) % 4
            src, dst = zs.at[mb, at, :, message_cols(g)], zr.at[mb, at, :, message_cols(g)]
            zc[mb, g, at] = remote(
                src, dst, zc_send.at[mb, g, at], zc_recv.at[mb, g, at], (section, tz * 4 + x))

    own_extra[...] = jnp.zeros_like(own_extra)
    for g in range(NG):
        from_gate[g].wait_recv()
        from_up[g].wait_recv()
        for c in range(*GROUPS[g]):
            rows = block_cols(c)
            keep(BWD, c, dot_t(act_a[...], gw[rows]) + dot_t(act_b[...], uw[rows]), None)
        if g + W_AHEAD < NG:
            send_weights(g + W_AHEAD)
        send_part(BWD, g, None)
        if g >= B_LAG:
            send_sum(BWD, g - B_LAG, None)
    if not F_OWN_EARLY:
        pass_rows(FWD, 0)
    for at in range(1, 4):
        pass_rows(FWD, at)
    for g in range(max(NG - B_LAG, 0), NG):
        send_sum(BWD, g, None)

    for half in range(2):
        for at in (2 * half, 2 * half + 1):
            wait_rows(FWD, at)
        acc_a[:144] = jnp.zeros((144, 256), F32)
        acc_b[:144] = jnp.zeros((144, 256), F32)
        for c in range(NBLK):
            rows = rows_of(FWD, c, half)
            acc_a[:144] += dot(rows, gw[block_cols(c)])
            acc_b[:144] += dot(rows, uw[block_cols(c)])
        act_a[:144] = (jax.nn.silu(acc_a[:144]) * acc_b[:144]).astype(BF16)
        own_extra[...] = jnp.zeros_like(own_extra)
        for g in range(NG):
            for c in range(*GROUPS[g]):
                keep(FWD, c, dot(act_a[:144], dw[:, block_cols(c)]), half)
            send_part(FWD, g, half)
        for g in range(NG):
            send_sum(FWD, g, half)

    def place(mb, out):
        infos[mb].wait_recv()
        info = info_r[mb]
        index = info[:, 0:1]
        def first_row(at):
            step = ((at & 1) << 1) | (at >> 1)
            return (((z + step) & 3) >> 1) * CAP

        col = iota((TOK, 128), 1)
        whole = (index == (first_row(col >> 5) + (col & 31)).astype(F32)).astype(BF16)
        extra_id = first_row(col >> 5) + 32 + (col & 1)
        for g in range(NG):
            for at in range(4):
                zc[mb, g, at].wait_recv()
        packed = zr[mb, :, :, TAIL].reshape(128, HALF)
        for c in range(NBLK):
            value = dot(whole, zr[mb, :, :, block_cols(c)].reshape(128, BLK))
            extra = []
            for up in (0, 8):
                wanted = jnp.where(((col & 31) >> 1) == c + up, extra_id, -1).astype(F32)
                extra.append(dot((index == wanted).astype(BF16), packed))
            value += jnp.concatenate(extra, axis=1)
            if mb == FWD:
                value = info[:, 1:2] * value
            out[0, :, block_cols(c)] = value.astype(BF16)

    place(BWD, out_b)
    place(FWD, out_f)
    for copy in sends:
        copy.wait_send()


def per_device(fi, fr, fw, bg, br, bw, saved, gate, up, down):
    vmem = pl.BlockSpec(memory_space=pltpu.VMEM)
    hbm = pl.BlockSpec(memory_space=pltpu.HBM)
    dma = pltpu.SemaphoreType.DMA
    rows_out = pltpu.VMEM((1, TOK, D), BF16)
    saved = saved[0].transpose(0, 2, 1, 3)
    fr, br = fr.reshape(1, TOK), br.reshape(1, TOK)
    return pl.pallas_call(
        kernel,
        out_shape=(rows_out, rows_out),
        in_specs=[hbm] * 10,
        out_specs=(vmem, vmem),
        scratch_shapes=[
            pltpu.VMEM((1, TOK, D), BF16),
            pltpu.VMEM((1, TOK), jnp.int32),
            pltpu.VMEM((1, TOK), F32),
            pltpu.VMEM((1, TOK, D), BF16),
            pltpu.VMEM((1, TOK), jnp.int32),
            pltpu.VMEM((1, TOK), F32),
            pltpu.VMEM((D, 2 * UNITS), BF16),
            pltpu.VMEM((D, 2 * UNITS), BF16),
            pltpu.VMEM((2 * UNITS, D), BF16),
            pltpu.VMEM((2, CAP, 16, UNITS), BF16),
            pltpu.VMEM((2, 272, 256), BF16),
            pltpu.VMEM((2, 272, UNITS), BF16),
            pltpu.VMEM((2, 2, 32, WIDE), BF16),
            pltpu.VMEM((2, 2, 4, 32, WIDE), BF16),
            pltpu.VMEM((2, TOK, 128), F32),
            pltpu.VMEM((2, TOK, 128), F32),
            pltpu.VMEM((272, 256), F32),
            pltpu.VMEM((272, 256), F32),
            pltpu.VMEM((272, 256), BF16),
            pltpu.VMEM((272, 256), BF16),
            pltpu.VMEM((128, D), F32),
            pltpu.VMEM((128, BLK), F32),
            pltpu.VMEM((2, 4, 32, WIDE), BF16),
            pltpu.VMEM((2, 4, 32, WIDE), BF16),
            pltpu.VMEM((2, 4, 32, WIDE), BF16),
            pltpu.VMEM((2, 4, 32, WIDE), BF16),
            dma((10,)),
            dma((2 + 2 * NG,)),
            dma((2 + 2 * NG,)),
            dma((2,)),
            dma((2,)),
            dma((2, 3)),
            dma((2, 3)),
            dma((2, 4)),
            dma((2, 4)),
            dma((2, 2, NG)),
            dma((2, 2, NG)),
            dma((2, NG, 4)),
            dma((2, NG, 4)),
        ],
        compiler_params=pltpu.CompilerParams(
            collective_id=0, has_side_effects=True, vmem_limit_bytes=60 * 2**20
        ),
        name="routed_experts",
    )(fi, fr, fw, bg, br, bw, saved, gate, up, down)


def solution(mesh):
    placed = (
        P("pipe", "expert", None),
        P("pipe", "expert", None),
        P("pipe", "expert"),
        P("pipe", "expert", None),
        P("pipe", "expert", None),
        P("pipe", "expert"),
        P("pipe", None, None, None, "expert"),
        P("pipe", None, "expert"),
        P("pipe", None, "expert"),
        P("pipe", "expert", None),
    )
    return jax.shard_map(
        per_device,
        mesh=mesh,
        in_specs=placed,
        out_specs=(P("pipe", "expert", None), P("pipe", "expert", None)),
        check_vma=False,
    )
```

```python
import jax
import jax.numpy as jnp
from jax import lax
from jax.experimental import pallas as pl
from jax.experimental.pallas import tpu as pltpu
from jax.sharding import PartitionSpec as P

MESH = pl.DeviceIdType.MESH
BF16 = jnp.bfloat16
F32 = jnp.float32
CAP = 34
TOK = 64
D = 3584
UNITS = 128
BLK = 512
NBLK = D // BLK
HALF = BLK // 2
WIDE = D + HALF
TAIL = pl.ds(D, HALF)
GROUPS = ((0, 1), (1, 3), (3, 5), (5, 6), (6, 7))
NG = len(GROUPS)
FWD, BWD = 0, 1
STEPS = (0, 2, 1, 3)
W_FIRST = 2
W_AHEAD = 5
B_LAG = 2
F_OWN_EARLY = True


def iota(shape, dim):
    return lax.broadcasted_iota(jnp.int32, shape, dim)


def dot(a, b):
    return jnp.dot(a, b, preferred_element_type=F32)


def dot_t(a, b):
    return lax.dot_general(a, b, (((1,), (1,)), ((), ())), preferred_element_type=F32)


def group_cols(g):
    first, last = GROUPS[g]
    return pl.ds(first * BLK, (last - first) * BLK)


def message_cols(g):
    first, last = GROUPS[g]
    return pl.ds(first * BLK, (last - first) * BLK + (HALF if g == NG - 1 else 0))


def block_cols(c):
    return pl.ds(c * BLK, BLK)


def column(values):
    diagonal = iota((TOK, TOK), 0) == iota((TOK, TOK), 1)
    spread = jnp.where(diagonal, jnp.broadcast_to(values.astype(F32), (TOK, TOK)), 0.0)
    return jnp.broadcast_to(jnp.sum(spread, axis=1, keepdims=True), (TOK, 128))


def row_index(route):
    to_one = (route == 1).astype(F32)
    earlier = (iota((TOK, TOK), 1) < iota((TOK, TOK), 0)).astype(BF16)
    ones_before = dot(earlier, to_one.astype(BF16))
    place = iota((TOK, 128), 0).astype(F32)
    return jnp.where(route == 1, CAP + ones_before, place - ones_before)


def tokens_in_lanes(index):
    diagonal = iota((TOK, TOK), 0) == iota((TOK, TOK), 1)
    spread = jnp.where(diagonal, index[:, :TOK], 0.0).astype(BF16)
    return dot(jnp.ones((TOK, TOK), BF16), spread)


def extra_match(short, long, c, half):
    if half is None:
        source = short >> 1
    else:
        source = jnp.where(short < 8, ((short >> 2) << 2) + 2 * half + ((short >> 1) & 1), -1)
    return (((long >> 4) == source) & ((long & 15) == 2 * c + (short & 1))).astype(BF16)


def unpack_extra(c, packed):
    short, long = iota((16, packed.shape[0]), 0), iota((16, packed.shape[0]), 1)
    source = short >> 1
    place = 2 * c + (short & 1)
    parts = [
        dot((((long >> 5) == source) & ((long & 31) == place + up)).astype(BF16), packed)
        for up in (0, 16)
    ]
    return jnp.concatenate(parts, axis=1).astype(BF16)


def pack_extra(c, half):
    return extra_match(iota((128, 16), 1), iota((128, 16), 0), c, half)


def kernel(
    fi_in, fr_in, fw_in, bg_in, br_in, bw_in, saved, gate, up, down,
    out_f, out_b,
    fi, fr, fw, bg, br, bw,
    gw, uw, dw, sv, sv_rows, sv_send,
    ds_main, tok,
    info_s, info_r,
    acc_a, acc_b, act_a, act_b,
    own, own_extra,
    xs, xr, zs, zr,
    loc_sem,
    w_send, w_recv, i_send, i_recv,
    zd_send, zd_recv, xd_send, xd_recv,
    xc_send, xc_recv, zc_send, zc_recv,
):
    p = lax.axis_index("pipe")
    e = lax.axis_index("expert")
    z, x = e // 4, e % 4
    turn = 1 - 2 * ((x + p) % 2)
    x_w = (x + turn + 4) % 4
    x_t = (x - turn + 4) % 4
    weight_peer = (p, z * 4 + x_w)
    token_peer = (p, z * 4 + x_t)
    after, before = (p + 1) % 16, (p + 15) % 16

    barrier = pltpu.get_barrier_semaphore()
    peers = [weight_peer, token_peer]
    peers += [(p, ((z + dz) % 4) * 4 + x) for dz in range(1, 4)]
    peers += [(q, ((z + dz) % 4) * 4 + x) for q in (after, before) for dz in range(4)]
    for peer in peers:
        pl.semaphore_signal(barrier, inc=1, device_id=peer, device_id_type=MESH)

    sends = []

    def remote(src, dst, send, recv, peer):
        copy = pltpu.make_async_remote_copy(
            src_ref=src, dst_ref=dst, send_sem=send, recv_sem=recv,
            device_id=peer, device_id_type=MESH,
        )
        copy.start()
        sends.append(copy)
        return copy

    small = [
        pltpu.make_async_copy(src, dst, loc_sem.at[4 + i])
        for i, (src, dst) in enumerate(
            ((br_in, br), (bw_in, bw), (bg_in, bg), (fr_in, fr), (fw_in, fw), (fi_in, fi))
        )
    ]
    for copy in small:
        copy.start()
    local = [
        pltpu.make_async_copy(gate.at[0], gw.at[:, pl.ds(0, UNITS)], loc_sem.at[0]),
        pltpu.make_async_copy(up.at[0], uw.at[:, pl.ds(0, UNITS)], loc_sem.at[1]),
        pltpu.make_async_copy(down.at[0], dw.at[pl.ds(0, UNITS)], loc_sem.at[2]),
        pltpu.make_async_copy(saved, sv, loc_sem.at[3]),
    ]
    for copy in local:
        copy.start()

    def read_grad(c):
        return (grad_col[:, :1] * bg[0, :, block_cols(c)].astype(F32)).astype(BF16)

    def read_input(c):
        return fi[0, :, block_cols(c)]

    def pick_main(mb, by_lane, read, g):
        row = iota((TOK, TOK), 0)
        picker = (by_lane == ((row >> 5) * CAP + (row & 31)).astype(F32)).astype(BF16)
        for c in range(*GROUPS[g]):
            picked = dot(picker, read(c)).astype(BF16)
            ds_main[mb, 0, :, block_cols(c)] = picked[:32]
            ds_main[mb, 1, :, block_cols(c)] = picked[32:]

    def pick_extra(mb, by_lane, read):
        row = iota((32, TOK), 0)
        extra_id = (row >> 4) * CAP + 32 + (row & 1)
        extra = jnp.zeros((32, BLK), F32)
        for c in range(NBLK):
            wanted = jnp.where(((row & 15) >> 1) == c, extra_id, -1).astype(F32)
            extra += dot((by_lane[:32] == wanted).astype(BF16), read(c))
        extra = extra.astype(BF16)
        for k in range(2):
            ds_main[mb, k, 0:16, TAIL] = extra[16 * k:16 * k + 16, :HALF]
            ds_main[mb, k, 16:32, TAIL] = extra[16 * k:16 * k + 16, HALF:]
        tok[mb, 0, 0] = ds_main[mb, z // 2]

    zd = {}
    xd = {}

    def send_rows(mb, at):
        tz = (z + STEPS[at]) % 4
        zd[mb, at] = remote(
            ds_main.at[mb, tz // 2], tok.at[mb, 0, at],
            zd_send.at[mb, at - 1], zd_recv.at[mb, at - 1], (p, tz * 4 + x))

    def pass_rows(mb, at):
        if at > 0:
            zd[mb, at].wait_recv()
        xd[mb, at] = remote(
            tok.at[mb, 0, at], tok.at[mb, 1, at], xd_send.at[mb, at], xd_recv.at[mb, at], token_peer)

    def wait_rows(mb, at):
        xd[mb, at].wait_recv()

    from_gate, from_up = [], []

    def send_weights(g):
        cols = group_cols(g)
        from_gate.append(remote(
            gate.at[0, cols], gw.at[cols, pl.ds(UNITS, UNITS)],
            w_send.at[2 + g], w_recv.at[2 + g], weight_peer))
        from_up.append(remote(
            up.at[0, cols], uw.at[cols, pl.ds(UNITS, UNITS)],
            w_send.at[2 + NG + g], w_recv.at[2 + NG + g], weight_peer))

    for copy in small[:3]:
        copy.wait()
    index_b = row_index(column(br[...]))
    grad_col = column(bw[...])
    info_s[BWD] = index_b
    lanes_b = tokens_in_lanes(index_b)
    for g in range(NG):
        pick_main(BWD, lanes_b, read_grad, g)
    pick_extra(BWD, lanes_b, read_grad)
    pl.semaphore_wait(barrier, len(peers))
    from_down = remote(down.at[0], dw.at[pl.ds(UNITS, UNITS)], w_send.at[0], w_recv.at[0], weight_peer)
    for at in range(1, 4):
        send_rows(BWD, at)
    pass_rows(BWD, 0)

    for copy in local:
        copy.wait()
    row, col = iota((272, 544), 0), iota((272, 544), 1)
    late = row >= 256
    source = jnp.where(late, (row - 256) >> 1, row >> 5)
    slot = jnp.where(late, 32 + (row & 1), row & 31)
    step = ((source & 1) << 1) | ((source >> 1) & 1)
    holder = ((z + 4 - step) & 3) * 4
    in_slot = (col >> 4) == slot
    mine = holder + jnp.where(source >= 4, x_t, x) == (col & 15)
    theirs = holder + jnp.where(source >= 4, (x + 2) % 4, x_w) == (col & 15)
    for kind in range(2):
        stored = sv[kind].reshape(544, UNITS)
        sv_send[kind] = dot((in_slot & theirs).astype(BF16), stored).astype(BF16)
        sv_rows[kind, :, 0:UNITS] = dot((in_slot & mine).astype(BF16), stored).astype(BF16)
    from_saved = remote(
        sv_send, sv_rows.at[:, :, pl.ds(UNITS, UNITS)], w_send.at[1], w_recv.at[1], weight_peer)

    for copy in small[3:]:
        copy.wait()
    index_f = row_index(column(fr[...]))
    info_s[FWD] = jnp.where(iota((TOK, 128), 1) == 1, column(fw[...]), index_f)
    lanes_f = tokens_in_lanes(index_f)
    infos = [
        remote(info_s.at[FWD], info_r.at[FWD], i_send.at[FWD], i_recv.at[FWD], (after, e)),
        remote(info_s.at[BWD], info_r.at[BWD], i_send.at[BWD], i_recv.at[BWD], (before, e)),
    ]
    for g in range(NG):
        pick_main(FWD, lanes_f, read_input, g)
    pick_extra(FWD, lanes_f, read_input)

    for g in range(W_FIRST):
        send_weights(g)
    if F_OWN_EARLY:
        pass_rows(FWD, 0)
    pass_rows(BWD, 2)
    send_rows(FWD, 1)
    pass_rows(BWD, 3)
    send_rows(FWD, 2)
    send_rows(FWD, 3)
    pass_rows(BWD, 1)
    for g in range(W_FIRST, W_AHEAD):
        send_weights(g)

    def rows_of(mb, c, half):
        count = 4 if half is None else 2
        first = 2 * half if half else 0
        main = tok[mb, :, first:first + count, :, block_cols(c)].reshape(64 * count, BLK)
        packed = tok[mb, :, first:first + count, :, TAIL].reshape(64 * count, HALF)
        extra = unpack_extra(c, packed)
        return jnp.concatenate([main, extra], axis=0)

    from_down.wait_recv()
    acc_a[...] = jnp.zeros_like(acc_a)
    for at in range(4):
        wait_rows(BWD, at)
    for c in range(NBLK):
        acc_a[...] += dot_t(rows_of(BWD, c, None), dw[:, block_cols(c)])
    from_saved.wait_recv()
    for h in range(2):
        lanes = pl.ds(h * UNITS, UNITS)
        g_pre, u_pre = sv_rows[0, :, lanes].astype(F32), sv_rows[1, :, lanes].astype(F32)
        sig = jax.nn.sigmoid(g_pre)
        grad = acc_a[:, lanes]
        act_a[:, lanes] = (grad * u_pre * sig * (1.0 + g_pre * (1.0 - sig))).astype(BF16)
        act_b[:, lanes] = (grad * g_pre * sig).astype(BF16)

    xc, zc = {}, {}

    def span(half):
        return (0, 4) if half is None else (2 * half, 2)

    def keep(mb, c, value, half):
        first, count = span(half)
        rows = 32 * count
        own[32 * first:32 * first + rows, block_cols(c)] = value[:rows]
        xs[mb, first:first + count, :, block_cols(c)] = (
            value[rows:2 * rows].astype(BF16).reshape(count, 32, BLK))
        own_extra[...] += dot(pack_extra(c, half), value[2 * rows:].astype(BF16))

    def send_part(mb, g, half):
        first, count = span(half)
        some = pl.ds(first, count)
        if g == NG - 1:
            packed = own_extra[64 + 16 * first:64 + 16 * (first + count)].astype(BF16).reshape(count, 16, BLK)
            xs[mb, first:first + count, 0:16, TAIL] = packed[:, :, :HALF]
            xs[mb, first:first + count, 16:32, TAIL] = packed[:, :, HALF:]
        src, dst = xs.at[mb, some, :, message_cols(g)], xr.at[mb, some, :, message_cols(g)]
        h = half or 0
        xc[mb, g, h] = remote(src, dst, xc_send.at[mb, h, g], xc_recv.at[mb, h, g], token_peer)

    def send_sum(mb, g, half):
        section = after if mb == FWD else before
        first, count = span(half)
        xc[mb, g, half or 0].wait_recv()
        if g == NG - 1:
            packed = own_extra[16 * first:16 * (first + count)].reshape(count, 16, BLK)
            for top, lanes in ((0, slice(0, HALF)), (16, slice(HALF, BLK))):
                zs[mb, first:first + count, top:top + 16, TAIL] = (
                    packed[:, :, lanes] + xr[mb, first:first + count, top:top + 16, TAIL].astype(F32)
                ).astype(BF16)
        for c in range(*GROUPS[g]):
            cols = block_cols(c)
            zs[mb, first:first + count, :, cols] = (
                own[32 * first:32 * (first + count), cols].reshape(count, 32, BLK)
                + xr[mb, first:first + count, :, cols].astype(F32)
            ).astype(BF16)
        for at in (1, 2, 3, 0):
            if not first <= at < first + count:
                continue
            tz = (z + 4 - STEPS[at]) % 4
            src, dst = zs.at[mb, at, :, message_cols(g)], zr.at[mb, at, :, message_cols(g)]
            zc[mb, g, at] = remote(
                src, dst, zc_send.at[mb, g, at], zc_recv.at[mb, g, at], (section, tz * 4 + x))

    own_extra[...] = jnp.zeros_like(own_extra)
    for g in range(NG):
        from_gate[g].wait_recv()
        from_up[g].wait_recv()
        for c in range(*GROUPS[g]):
            rows = block_cols(c)
            keep(BWD, c, dot_t(act_a[...], gw[rows]) + dot_t(act_b[...], uw[rows]), None)
        if g + W_AHEAD < NG:
            send_weights(g + W_AHEAD)
        send_part(BWD, g, None)
        if g >= B_LAG:
            send_sum(BWD, g - B_LAG, None)
    if not F_OWN_EARLY:
        pass_rows(FWD, 0)
    for at in range(1, 4):
        pass_rows(FWD, at)
    for g in range(max(NG - B_LAG, 0), NG):
        send_sum(BWD, g, None)

    for half in range(2):
        for at in (2 * half, 2 * half + 1):
            wait_rows(FWD, at)
        acc_a[:144] = jnp.zeros((144, 256), F32)
        acc_b[:144] = jnp.zeros((144, 256), F32)
        for c in range(NBLK):
            rows = rows_of(FWD, c, half)
            acc_a[:144] += dot(rows, gw[block_cols(c)])
            acc_b[:144] += dot(rows, uw[block_cols(c)])
        act_a[:144] = (jax.nn.silu(acc_a[:144]) * acc_b[:144]).astype(BF16)
        own_extra[...] = jnp.zeros_like(own_extra)
        for g in range(NG):
            for c in range(*GROUPS[g]):
                keep(FWD, c, dot(act_a[:144], dw[:, block_cols(c)]), half)
            send_part(FWD, g, half)
        early = len(sends)
        for g in range(NG):
            send_sum(FWD, g, half)

    def place(mb, out):
        infos[mb].wait_recv()
        info = info_r[mb]
        index = info[:, 0:1]
        def first_row(at):
            step = ((at & 1) << 1) | (at >> 1)
            return (((z + step) & 3) >> 1) * CAP

        col = iota((TOK, 128), 1)
        whole = (index == (first_row(col >> 5) + (col & 31)).astype(F32)).astype(BF16)
        extra_id = first_row(col >> 5) + 32 + (col & 1)
        for g in range(NG):
            for at in range(4):
                zc[mb, g, at].wait_recv()
        packed = zr[mb, :, :, TAIL].reshape(128, HALF)
        for c in range(NBLK):
            value = dot(whole, zr[mb, :, :, block_cols(c)].reshape(128, BLK))
            extra = []
            for up in (0, 8):
                wanted = jnp.where(((col & 31) >> 1) == c + up, extra_id, -1).astype(F32)
                extra.append(dot((index == wanted).astype(BF16), packed))
            value += jnp.concatenate(extra, axis=1)
            if mb == FWD:
                value = info[:, 1:2] * value
            out[0, :, block_cols(c)] = value.astype(BF16)

    place(BWD, out_b)
    for copy in sends[:early]:
        copy.wait_send()
    place(FWD, out_f)
    for copy in sends[early:]:
        copy.wait_send()


def per_device(fi, fr, fw, bg, br, bw, saved, gate, up, down):
    vmem = pl.BlockSpec(memory_space=pltpu.VMEM)
    hbm = pl.BlockSpec(memory_space=pltpu.HBM)
    dma = pltpu.SemaphoreType.DMA
    rows_out = pltpu.VMEM((1, TOK, D), BF16)
    saved = saved[0].transpose(0, 2, 1, 3)
    fr, br = fr.reshape(1, TOK), br.reshape(1, TOK)
    return pl.pallas_call(
        kernel,
        out_shape=(rows_out, rows_out),
        in_specs=[hbm] * 10,
        out_specs=(vmem, vmem),
        scratch_shapes=[
            pltpu.VMEM((1, TOK, D), BF16),
            pltpu.VMEM((1, TOK), jnp.int32),
            pltpu.VMEM((1, TOK), F32),
            pltpu.VMEM((1, TOK, D), BF16),
            pltpu.VMEM((1, TOK), jnp.int32),
            pltpu.VMEM((1, TOK), F32),
            pltpu.VMEM((D, 2 * UNITS), BF16),
            pltpu.VMEM((D, 2 * UNITS), BF16),
            pltpu.VMEM((2 * UNITS, D), BF16),
            pltpu.VMEM((2, CAP, 16, UNITS), BF16),
            pltpu.VMEM((2, 272, 256), BF16),
            pltpu.VMEM((2, 272, UNITS), BF16),
            pltpu.VMEM((2, 2, 32, WIDE), BF16),
            pltpu.VMEM((2, 2, 4, 32, WIDE), BF16),
            pltpu.VMEM((2, TOK, 128), F32),
            pltpu.VMEM((2, TOK, 128), F32),
            pltpu.VMEM((272, 256), F32),
            pltpu.VMEM((272, 256), F32),
            pltpu.VMEM((272, 256), BF16),
            pltpu.VMEM((272, 256), BF16),
            pltpu.VMEM((128, D), F32),
            pltpu.VMEM((128, BLK), F32),
            pltpu.VMEM((2, 4, 32, WIDE), BF16),
            pltpu.VMEM((2, 4, 32, WIDE), BF16),
            pltpu.VMEM((2, 4, 32, WIDE), BF16),
            pltpu.VMEM((2, 4, 32, WIDE), BF16),
            dma((10,)),
            dma((2 + 2 * NG,)),
            dma((2 + 2 * NG,)),
            dma((2,)),
            dma((2,)),
            dma((2, 3)),
            dma((2, 3)),
            dma((2, 4)),
            dma((2, 4)),
            dma((2, 2, NG)),
            dma((2, 2, NG)),
            dma((2, NG, 4)),
            dma((2, NG, 4)),
        ],
        compiler_params=pltpu.CompilerParams(
            collective_id=0, has_side_effects=True, vmem_limit_bytes=60 * 2**20
        ),
        name="routed_experts",
    )(fi, fr, fw, bg, br, bw, saved, gate, up, down)


def solution(mesh):
    placed = (
        P("pipe", "expert", None),
        P("pipe", "expert", None),
        P("pipe", "expert"),
        P("pipe", "expert", None),
        P("pipe", "expert", None),
        P("pipe", "expert"),
        P("pipe", None, None, None, "expert"),
        P("pipe", None, "expert"),
        P("pipe", None, "expert"),
        P("pipe", "expert", None),
    )
    return jax.shard_map(
        per_device,
        mesh=mesh,
        in_specs=placed,
        out_specs=(P("pipe", "expert", None), P("pipe", "expert", None)),
        check_vma=False,
    )
```
